256 devices in a mesh: img: 4 (over x_lo, core), txt: 64 (over y, z, x_hi).
Axes of the slice: x: 4 (x_hi: 2, x_lo: 2; x = x_hi * 2 + x_lo), y: 4, z: 8, core: 2. Of those that a mesh axis runs over, the one named last changes fastest.
Arguments:
- images: bfloat16 [14336, 1280], P(('img', 'txt')), may hold values from -128 to 128
- texts: bfloat16 [14336, 1280], P(('txt', 'img')), may hold values from -16 to 16
- logit_scale: float32 [1], replicated, may hold values from 0.02 to 0.04
Outputs:
- loss: float32 [1], replicated
- image_grad: float32 [14336, 1280], P(('img', 'txt'))
- text_grad: float32 [14336, 1280], P(('txt', 'img'))
The draws below stay inside these ranges and needn't reach their ends.
All inputs are finite; a program needn't handle non-finite values.
Results may differ from the reference program's by a relative error of at most 0.0021.
Values may be sent and summed in bfloat16 or wider, within the bound.
A program may use at most 64 MiB of HBM per device.

```python
import math
import jax
import jax.numpy as jnp
from jax import lax

E = 1280
PAIRS = 14336


def pair_fields(key, spike_rate):
    key_text, key_noise, key_tscale, key_iscale, key_pick, key_strength, key_spike = jax.random.split(key, 7)
    field_shape = (PAIRS, E)
    base_text = jax.random.normal(key_text, field_shape, jnp.float32)
    base_noise = jax.random.normal(key_noise, field_shape, jnp.float32)
    text_scale = jnp.exp(jax.random.uniform(key_tscale, (PAIRS, 1), jnp.float32, -0.55, 0.55))
    image_scale = jnp.exp(jax.random.uniform(key_iscale, (PAIRS, 1), jnp.float32, -0.55, 0.55))
    text_field = base_text * text_scale
    image_field = (0.12 * base_text + base_noise) * image_scale
    picked = jax.random.uniform(key_pick, (PAIRS,), jnp.float32) < spike_rate
    levels = jnp.array([110.0, 180.0, 260.0], jnp.float32)
    target = levels[jax.random.randint(key_strength, (PAIRS,), 0, 3)]
    spike_text = 3.0 * jax.random.uniform(key_spike, field_shape, jnp.float32, -1.7, 1.7)
    text_field = jnp.where(picked[:, None], spike_text, text_field)
    before = jnp.roll(picked, 1)
    text_field = jnp.where(before[:, None], 0.985 * jnp.roll(text_field, 1, 0), text_field)
    factor = target / (0.03 * E * 9.0 * 0.963)
    image_field = jnp.where(picked[:, None], factor[:, None] * text_field, image_field)
    return (image_field, text_field)


def draw_images(key, part):
    return pair_fields(key, 1.0 / 64.0)[0].astype(jnp.bfloat16)


def draw_texts(key, part):
    return pair_fields(key, 1.0 / 64.0)[1].astype(jnp.bfloat16)


def setup_inputs(seed: int = 0) -> dict:
    keys = jax.random.split(jax.random.key(seed), 4)
    return {
        "images": draw_images(jax.random.fold_in(keys[3], 71), 0),
        "texts": draw_texts(jax.random.fold_in(keys[3], 71), 0),
        "logit_scale": jnp.clip(jnp.exp(jax.random.uniform(keys[2], (1,), jnp.float32, math.log(0.02), math.log(0.04))), 0.02, 0.04),
    }


def reference(images, texts, logit_scale):
    scale = logit_scale[0]
    pairs = images.shape[0]
    block = math.gcd(pairs, 512)
    count = pairs // block
    image_blocks = images.reshape(count, block, images.shape[1])

    def block_logits(row_block):
        return scale * lax.dot_general(row_block, texts, (((1,), (1,)), ((), ())), preferred_element_type=jnp.float32)

    def first_pass(carry, row_block):
        col_peak, col_total = carry
        logits = block_logits(row_block)
        row_peak = jnp.max(logits, 1)
        row_total = jnp.sum(jnp.exp(logits - row_peak[:, None]), 1)
        new_peak = jnp.maximum(col_peak, jnp.max(logits, 0))
        col_total = col_total * jnp.exp(col_peak - new_peak) + jnp.sum(jnp.exp(logits - new_peak[None, :]), 0)
        return (new_peak, col_total), (row_peak, row_total)

    start = (jnp.full((pairs,), -jnp.inf, jnp.float32), jnp.zeros((pairs,), jnp.float32))
    (col_peak, col_total), (row_peak, row_total) = lax.scan(first_pass, start, image_blocks)
    row_peak = row_peak.reshape(count, block)
    row_total = row_total.reshape(count, block)
    col_index = jnp.arange(pairs, dtype=jnp.int32)

    def second_pass(text_acc, inputs):
        row_block, peak_block, total_block, number = inputs
        logits = block_logits(row_block)
        row_prob = jnp.exp(logits - peak_block[:, None]) / total_block[:, None]
        col_prob = jnp.exp(logits - col_peak[None, :]) / col_total[None, :]
        row_index = number * block + jnp.arange(block, dtype=jnp.int32)
        on_diagonal = row_index[:, None] == col_index[None, :]
        weights = (0.5 * (row_prob + col_prob) - jnp.where(on_diagonal, 1.0, 0.0)).astype(jnp.bfloat16)
        image_part = jnp.dot(weights, texts, preferred_element_type=jnp.float32)
        text_acc = text_acc + lax.dot_general(weights, row_block, (((0,), (0,)), ((), ())), preferred_element_type=jnp.float32)
        return text_acc, image_part

    numbers = jnp.arange(count, dtype=jnp.int32)
    text_grad, image_parts = lax.scan(second_pass, jnp.zeros(texts.shape, jnp.float32), (image_blocks, row_peak, row_total, numbers))
    image_grad = image_parts.reshape(images.shape)
    diagonal = scale * jnp.sum(images.astype(jnp.float32) * texts.astype(jnp.float32), 1)
    total = jnp.sum(row_peak + jnp.log(row_total)) + jnp.sum(col_peak + jnp.log(col_total)) - 2.0 * jnp.sum(diagonal)
    loss = jnp.reshape(total / (2.0 * pairs), (1,))
    return loss, image_grad, text_grad
```

```python
import functools

import jax
import jax.numpy as jnp
from jax import lax
from jax.experimental import pallas as pl
from jax.experimental.pallas import tpu as pltpu
from jax.sharding import PartitionSpec as P

MESH = pl.DeviceIdType.MESH
ROWS = 56
PITCH = 64
SIDE = 16
TILE = SIDE * PITCH
E = 1280
PAIRS = 14336
WIDE = 256
FLOOR = -1e30
PIECES = (
    (0, 0, 256, 0),
    (1, 256, 256, 0),
    (0, 512, 256, 256),
    (1, 768, 256, 256),
    (0, 1024, 128, 512),
    (1, 1152, 128, 512),
)
HALF = 640


def device(x, y, z, c):
    return (lax.rem(x, 2) * 2 + c, (y * 8 + z) * 2 + lax.div(x, 2))


def kernel(
    images_ref, texts_ref, scale_ref,
    loss_ref, igrad_ref, tgrad_ref,
    ibuf, tbuf, ibig, tbig, logits, prow, pcol, weights, wturned,
    rsub, csum, cmax, dsum, frow, rmsg, cmsg, rstats, cstats, lmsg, lstats, pmsg, pstats,
    xout, xin, zacc, zout, zin, tacc, sout, sin, pout, pin, pkeep,
    zsend, isend, irecv, tsend0, trecv, tsend1,
    rsend, rrecv, csend, crecv, lsend, lrecv, psend, precv,
    xsend, xrecv, zosend, zorecv, ssend, srecv, ppsend, pprecv,
):
    img = lax.axis_index("img")
    txt = lax.axis_index("txt")
    x_lo = lax.div(img, 2)
    c = lax.rem(img, 2)
    x_hi = lax.rem(txt, 2)
    x = x_hi * 2 + x_lo
    y = lax.div(txt, 16)
    z = lax.rem(lax.div(txt, 2), 8)
    oc = 1 - c
    islot = c * 8 + z
    tslot = x * 4 + y

    def row_peer(slot):
        return device(x, y, lax.rem(slot, 8), lax.div(slot, 8))

    def col_peer(slot):
        return device(lax.div(slot, 4), lax.rem(slot, 4), z, c)

    def copy(src, dst, send, recv, where):
        return pltpu.make_async_remote_copy(
            src_ref=src, dst_ref=dst, send_sem=send, recv_sem=recv,
            device_id=where, device_id_type=MESH,
        )

    barrier = pltpu.get_barrier_semaphore()

    def greet(k, carry):
        pl.semaphore_signal(barrier, inc=1, device_id=row_peer(lax.rem(islot + k, SIDE)), device_id_type=MESH)
        pl.semaphore_signal(barrier, inc=1, device_id=col_peer(lax.rem(tslot + k, SIDE)), device_id_type=MESH)
        return carry

    lax.fori_loop(1, SIDE, greet, 0)
    ibuf[islot] = images_ref[...]
    tbuf[tslot] = texts_ref[...]
    ibig[...] = jnp.zeros_like(ibig)
    tbig[...] = jnp.zeros_like(tbig)
    weights[...] = jnp.zeros_like(weights)
    rsub[...] = jnp.zeros_like(rsub)
    pl.semaphore_wait(barrier, 2 * (SIDE - 1))

    def z_copy(owner, way, step):
        slot = c * 8 + owner
        there = lax.rem(z + (1 if way == 0 else 7), 8)
        return copy(ibuf.at[slot], ibuf.at[slot], zsend.at[way, step], irecv.at[slot], device(x, y, there, c))

    def cross_copy(slot, k):
        return copy(ibuf.at[slot], ibuf.at[slot], isend.at[k], irecv.at[slot], device(x, y, z, oc))

    def wait_image(slot):
        copy(ibuf.at[slot], ibuf.at[slot], isend.at[0], irecv.at[slot], device(x, y, z, oc)).wait_recv()

    def whole_copy(axis, d):
        there = device(lax.rem(x + d, 4), y, z, c) if axis == 0 else device(x, lax.rem(y + d, 4), z, c)
        return copy(tbuf.at[tslot], tbuf.at[tslot], tsend0.at[axis, d], trecv.at[0, tslot], there)

    def wait_whole(slot):
        copy(tbuf.at[slot], tbuf.at[slot], tsend0.at[0, 0], trecv.at[0, slot], device(x, y, z, oc)).wait_recv()

    def half_ref(slot, half):
        return tbuf.at[slot, :, pl.ds(half * HALF, HALF)]

    def half_copy(half, d, e):
        if half == 0:
            slot = lax.rem(x + d, 4) * 4 + y
            there = device(x, lax.rem(y + e, 4), z, c)
        else:
            slot = x * 4 + lax.rem(y + d, 4)
            there = device(lax.rem(x + e, 4), y, z, c)
        return copy(half_ref(slot, half), half_ref(slot, half), tsend1.at[half, d * 4 + e], trecv.at[half, slot], there)

    def wait_half(slot, half):
        copy(half_ref(slot, half), half_ref(slot, half), tsend0.at[0, 0], trecv.at[half, slot], device(x, y, z, oc)).wait_recv()

    z_copy(z, 0, 0).start()
    z_copy(z, 1, 0).start()
    for d in (1, 3, 2):
        whole_copy(0, d).start()
        whole_copy(1, d).start()
    cross_copy(islot, 0).start()

    def place_image(slot):
        at = pl.multiple_of(slot * PITCH, PITCH)
        ibig[pl.ds(at, ROWS), :] = ibuf[slot]

    def place_text(slot):
        at = pl.multiple_of(slot * PITCH, PITCH)
        tbig[pl.ds(at, ROWS), :] = tbuf[slot]

    place_image(islot)
    place_text(tslot)
    for step in range(3):
        left = lax.rem(z + 7 - step, 8)
        right = lax.rem(z + 1 + step, 8)
        wait_image(c * 8 + left)
        if step < 2:
            z_copy(left, 0, step + 1).start()
        else:
            @pl.when(c == 0)
            def _():
                z_copy(left, 0, 3).start()
        cross_copy(c * 8 + left, 1 + step).start()
        wait_image(c * 8 + right)
        if step < 2:
            z_copy(right, 1, step + 1).start()
        else:
            @pl.when(c == 1)
            def _():
                z_copy(right, 1, 3).start()
        cross_copy(c * 8 + right, 4 + step).start()
        d = (1, 3, 2)[step]
        slot0 = lax.rem(x + d, 4) * 4 + y
        slot1 = x * 4 + lax.rem(y + d, 4)
        wait_whole(slot0)
        wait_whole(slot1)
        for e in (1, 3, 2):
            half_copy(0, d, e).start()
            half_copy(1, d, e).start()
        place_image(c * 8 + left)
        place_image(c * 8 + right)
        place_text(slot0)
        place_text(slot1)
    far = lax.rem(z + 4, 8)
    wait_image(c * 8 + far)
    cross_copy(c * 8 + far, 7).start()
    place_image(c * 8 + far)
    for d in (1, 3, 2):
        for e in (1, 3, 2):
            slot = lax.rem(x + d, 4) * 4 + lax.rem(y + e, 4)
            wait_half(slot, 0)
            wait_half(slot, 1)
            place_text(slot)

    def other_image(k, carry):
        slot = oc * 8 + k
        wait_image(slot)
        place_image(slot)
        return carry

    lax.fori_loop(0, 8, other_image, 0)

    scale = scale_ref[0]
    lane = lax.broadcasted_iota(jnp.int32, (1, TILE), 1)
    inside = lax.bitwise_and(lane, PITCH - 1)
    block = lax.shift_right_logical(lane, 6)
    block_x = lax.shift_right_logical(block, 2)
    block_y = lax.bitwise_and(block, 3)
    col_block = ((block_y * 8 + z) * 2 + lax.shift_right_logical(block_x, 1)) * 4 + lax.bitwise_and(block_x, 1) * 2 + c
    col_id = jnp.where(inside < ROWS, col_block * ROWS + inside, -1)

    def score(n, carry):
        cols = pl.ds(pl.multiple_of(n * WIDE, WIDE), WIDE)
        part = lax.dot_general(
            ibig[...], tbig[cols, :], (((1,), (1,)), ((), ())), preferred_element_type=jnp.float32
        )
        pad = lax.bitwise_and(lax.broadcasted_iota(jnp.int32, (1, WIDE), 1), PITCH - 1) >= ROWS
        logits[:, cols] = jnp.where(pad, FLOOR, part * scale)
        return carry

    lax.fori_loop(0, TILE // WIDE, score, 0)

    def rows_of(k):
        return pl.ds(pl.multiple_of(k * PITCH, PITCH), ROWS)

    cmax[...] = jnp.full_like(cmax, FLOOR)

    def col_max(k, carry):
        cmax[...] = jnp.maximum(cmax[...], jnp.max(logits[rows_of(k), :].reshape(7, 8, TILE), 0))
        return carry

    lax.fori_loop(0, SIDE, col_max, 0)
    col_top = jnp.max(cmax[...], 0, keepdims=True)
    csum[...] = jnp.zeros_like(csum)
    dsum[...] = jnp.zeros_like(dsum)

    def on_diagonal(k):
        row_block = (x_lo * 2 + lax.div(k, 8)) * 64 + (y * 8 + lax.rem(k, 8)) * 2 + x_hi
        row_id = row_block * ROWS + lax.broadcasted_iota(jnp.int32, (ROWS, 1), 0)
        return row_id == col_id

    def exponentials(k, carry):
        part = logits[rows_of(k), :]
        top = jnp.max(part, 1, keepdims=True)
        by_row = jnp.exp(part - top)
        by_col = jnp.exp(part - col_top)
        prow[rows_of(k), :] = by_row
        pcol[rows_of(k), :] = by_col
        total = jnp.sum(by_row, 1, keepdims=True)
        first = lax.broadcasted_iota(jnp.int32, (ROWS, 128), 1) == 0
        rsub[rows_of(k), :] = jnp.where(first, top, total)
        csum[...] += jnp.sum(by_col.reshape(7, 8, TILE), 0)
        dsum[...] += jnp.sum(jnp.where(on_diagonal(k), part, 0.0).reshape(7, 8, TILE), 0)
        return carry

    lax.fori_loop(0, SIDE, exponentials, 0)

    row_stats = jnp.transpose(rsub[...], (1, 0))
    col_total_here = jnp.sum(csum[...], 0, keepdims=True)
    for k in range(4):
        part = slice(k * WIDE, (k + 1) * WIDE)
        rmsg[k:k + 1, :] = row_stats[0:1, part]
        rmsg[4 + k:5 + k, :] = row_stats[1:2, part]
        cmsg[k:k + 1, :] = col_top[:, part]
        cmsg[4 + k:5 + k, :] = col_total_here[:, part]
    rstats[islot] = rmsg[...]
    cstats[tslot] = cmsg[...]

    def row_stat_copy(peer):
        return copy(rmsg, rstats.at[islot], rsend.at[peer], rrecv.at[islot], row_peer(peer))

    def col_stat_copy(peer):
        return copy(cmsg, cstats.at[tslot], csend.at[peer], crecv.at[tslot], col_peer(peer))

    def send_stats(k, carry):
        row_stat_copy(lax.rem(islot + k, SIDE)).start()
        col_stat_copy(lax.rem(tslot + k, SIDE)).start()
        return carry

    lax.fori_loop(1, SIDE, send_stats, 0)

    def take_stats(k, carry):
        peer = lax.rem(islot + k, SIDE)
        copy(rmsg, rstats.at[peer], rsend.at[peer], rrecv.at[peer], row_peer(peer)).wait_recv()
        peer = lax.rem(tslot + k, SIDE)
        copy(cmsg, cstats.at[peer], csend.at[peer], crecv.at[peer], col_peer(peer)).wait_recv()
        return carry

    lax.fori_loop(1, SIDE, take_stats, 0)

    def combine(stats, mine):
        peaks = stats[:, 0:4, :]
        totals = stats[:, 4:8, :]
        peak = jnp.max(peaks, 0)
        total = jnp.sum(totals * jnp.exp(peaks - peak[None]), 0)
        factor = 0.5 * jnp.exp(mine[0:4, :] - peak) / total
        return peak + jnp.log(total), factor

    row_lse, row_factor = combine(rstats, rmsg)
    col_lse, col_factor = combine(cstats, cmsg)

    def line(v):
        return jnp.concatenate([v[k:k + 1, :] for k in range(4)], 1)

    col_line = line(col_factor)
    frow[...] = jnp.transpose(jnp.broadcast_to(line(row_factor), (128, TILE)), (1, 0))

    def weigh(k, carry):
        factor = frow[rows_of(k), :][:, 0:1]
        w = factor * prow[rows_of(k), :] + col_line * pcol[rows_of(k), :]
        w = w - jnp.where(on_diagonal(k), 1.0, 0.0)
        weights[rows_of(k), :] = w.astype(jnp.bfloat16)
        return carry

    lax.fori_loop(0, SIDE, weigh, 0)

    def cross_term(n):
        cols = pl.ds(pl.multiple_of(n * WIDE, WIDE), WIDE)
        return copy(xout.at[:, :, cols], xin.at[:, :, cols], xsend.at[n], xrecv.at[n], device(x, y, z, oc))

    def other_terms(n, carry):
        cols = pl.ds(pl.multiple_of(n * WIDE, WIDE), WIDE)
        at = pl.multiple_of(oc * (8 * PITCH), 8 * PITCH)
        part = jnp.dot(weights[pl.ds(at, 8 * PITCH), :], tbig[:, cols], preferred_element_type=jnp.float32)
        for m in range(8):
            xout[m, :, cols] = part[m * PITCH:m * PITCH + ROWS]
        cross_term(n).start()
        return carry

    lax.fori_loop(0, E // WIDE, other_terms, 0)

    def z_term(n, d):
        cols = pl.ds(pl.multiple_of(n * WIDE, WIDE), WIDE)
        there = lax.rem(z + d, 8)
        return copy(zout.at[there, :, cols], zin.at[z, :, cols], zosend.at[n, d], zorecv.at[n, z], device(x, y, there, c))

    def z_wait(n, d):
        cols = pl.ds(pl.multiple_of(n * WIDE, WIDE), WIDE)
        src = lax.rem(z + d, 8)
        copy(zin.at[src, :, cols], zin.at[src, :, cols], zosend.at[n, d], zorecv.at[n, src], device(x, y, z, oc)).wait_recv()

    def own_terms(n, carry):
        cols = pl.ds(pl.multiple_of(n * WIDE, WIDE), WIDE)
        at = pl.multiple_of(c * (8 * PITCH), 8 * PITCH)
        part = jnp.dot(weights[pl.ds(at, 8 * PITCH), :], tbig[:, cols], preferred_element_type=jnp.float32)
        cross_term(n).wait_recv()
        for m in range(8):
            both = part[m * PITCH:m * PITCH + ROWS] + xin[m, :, cols]
            zacc[m, :, cols] = both
            zout[m, :, cols] = both.astype(jnp.bfloat16)
        for d in (4, 3, 5, 2, 6, 1, 7):
            z_term(n, d).start()
        return carry

    lax.fori_loop(0, E // WIDE, own_terms, 0)

    for k in range(TILE // 128):
        wturned[:, k * 128:(k + 1) * 128] = jnp.transpose(weights[k * 128:(k + 1) * 128, :], (1, 0))

    def first_peer(axis, f):
        return device(x, f, z, c) if axis == 0 else device(f, y, z, c)

    def second_peer(axis, s):
        return device(s, y, z, c) if axis == 0 else device(x, s, z, c)

    def slab_copy(p, d):
        axis, _, width, at = PIECES[p]
        me = y if axis == 0 else x
        there = lax.rem(me + d, 4)
        return copy(
            sout.at[axis, there, :, :, pl.ds(at, width)], sin.at[axis, me, :, :, pl.ds(at, width)],
            ssend.at[p, d], srecv.at[p, me], first_peer(axis, there),
        )

    def slab_wait(p, d):
        axis, _, width, at = PIECES[p]
        me = y if axis == 0 else x
        src = lax.rem(me + d, 4)
        ref = sin.at[axis, src, :, :, pl.ds(at, width)]
        copy(ref, ref, ssend.at[p, d], srecv.at[p, src], first_peer(axis, src)).wait_recv()

    for n in range(E // WIDE):
        part = jnp.dot(wturned[...], ibig[:, n * WIDE:(n + 1) * WIDE], preferred_element_type=jnp.float32)
        for p, (axis, col, width, at) in enumerate(PIECES):
            if col // WIDE != n:
                continue
            for m in range(SIDE):
                piece = part[m * PITCH:m * PITCH + ROWS, col - n * WIDE:col - n * WIDE + width]
                tacc[m, :, col:col + width] = piece
                first, second = (m % 4, m // 4) if axis == 0 else (m // 4, m % 4)
                sout[axis, first, second, :, at:at + width] = piece.astype(jnp.bfloat16)
            for d in (2, 1, 3):
                slab_copy(p, d).start()

    index = lax.broadcasted_iota(jnp.int32, (4, WIDE), 0) * WIDE + lax.broadcasted_iota(jnp.int32, (4, WIDE), 1)
    slot_of = lax.shift_right_logical(index, 6)
    valid = lax.bitwise_and(index, PITCH - 1) < ROWS
    terms = jnp.where(valid & (slot_of == islot), row_lse, 0.0) + jnp.where(valid & (slot_of == tslot), col_lse, 0.0)
    term = jnp.sum(jnp.sum(terms, 0, keepdims=True), 1, keepdims=True)
    diagonal = jnp.sum(jnp.sum(dsum[...], 0, keepdims=True), 1, keepdims=True)
    lmsg[...] = jnp.broadcast_to(term - 2.0 * diagonal, (8, 128))
    lstats[islot] = lmsg[...]

    def send_loss(k, carry):
        peer = lax.rem(islot + k, SIDE)
        copy(lmsg, lstats.at[islot], lsend.at[peer], lrecv.at[islot], row_peer(peer)).start()
        return carry

    lax.fori_loop(1, SIDE, send_loss, 0)

    def keep_copy(p, d):
        axis, _, width, at = PIECES[p]
        me = x if axis == 0 else y
        there = lax.rem(me + d, 4)
        return copy(
            pout.at[axis, there, :, pl.ds(at, width)], pin.at[axis, me, :, pl.ds(at, width)],
            ppsend.at[p, d], pprecv.at[p, me], second_peer(axis, there),
        )

    for p, (axis, col, width, at) in enumerate(PIECES):
        for d in (1, 3, 2):
            slab_wait(p, d)
        me1 = y if axis == 0 else x
        me2 = x if axis == 0 else y
        for d in (2, 1, 3, 0):
            s = lax.rem(me2 + d, 4)
            m = s * 4 + y if axis == 0 else x * 4 + s
            total = tacc[m, :, col:col + width]
            for e in (1, 2, 3):
                f = lax.rem(me1 + e, 4)
                total = total + sin[axis, f, s, :, at:at + width].astype(jnp.float32)
            if d == 0:
                pkeep[:, col:col + width] = total
            else:
                pout[axis, s, :, at:at + width] = total.astype(jnp.bfloat16)
                keep_copy(p, d).start()

    def take_loss(k, carry):
        peer = lax.rem(islot + k, SIDE)
        copy(lmsg, lstats.at[peer], lsend.at[peer], lrecv.at[peer], row_peer(peer)).wait_recv()
        return carry

    lax.fori_loop(1, SIDE, take_loss, 0)
    pmsg[...] = jnp.sum(lstats[...], 0)
    pstats[tslot] = pmsg[...]

    def send_sum(k, carry):
        peer = lax.rem(tslot + k, SIDE)
        copy(pmsg, pstats.at[tslot], psend.at[peer], precv.at[tslot], col_peer(peer)).start()
        return carry

    lax.fori_loop(1, SIDE, send_sum, 0)

    for p, (axis, col, width, at) in enumerate(PIECES):
        me = x if axis == 0 else y
        total = pkeep[:, col:col + width]
        for d in (1, 3, 2):
            src = lax.rem(me + d, 4)
            ref = pin.at[axis, src, :, pl.ds(at, width)]
            copy(ref, ref, ppsend.at[p, d], pprecv.at[p, src], second_peer(axis, src)).wait_recv()
            total = total + pin[axis, src, :, at:at + width].astype(jnp.float32)
        tgrad_ref[:, col:col + width] = total

    def image_result(n, carry):
        cols = pl.ds(pl.multiple_of(n * WIDE, WIDE), WIDE)
        total = zacc[z, :, cols]
        for d in (1, 7, 2, 6, 3, 5, 4):
            z_wait(n, d)
            total = total + zin[lax.rem(z + d, 8), :, cols].astype(jnp.float32)
        igrad_ref[:, cols] = total
        return carry

    lax.fori_loop(0, E // WIDE, image_result, 0)

    def take_sum(k, carry):
        peer = lax.rem(tslot + k, SIDE)
        copy(pmsg, pstats.at[peer], psend.at[peer], precv.at[peer], col_peer(peer)).wait_recv()
        return carry

    lax.fori_loop(1, SIDE, take_sum, 0)
    loss = jnp.sum(pstats[...], 0) / (2.0 * PAIRS)
    loss_ref[0] = loss[0, 0]

    for way in range(2):
        for step in range(3):
            z_copy(z, way, step).wait_send()

    @pl.when(c == 0)
    def _():
        z_copy(z, 0, 3).wait_send()

    @pl.when(c == 1)
    def _():
        z_copy(z, 1, 3).wait_send()

    for k in range(8):
        cross_copy(islot, k).wait_send()
    for d in (1, 3, 2):
        whole_copy(0, d).wait_send()
        whole_copy(1, d).wait_send()
        for e in (1, 3, 2):
            half_copy(0, d, e).wait_send()
            half_copy(1, d, e).wait_send()

    def sent(k, carry):
        peer = lax.rem(islot + k, SIDE)
        row_stat_copy(peer).wait_send()
        copy(lmsg, lstats.at[islot], lsend.at[peer], lrecv.at[islot], row_peer(peer)).wait_send()
        peer = lax.rem(tslot + k, SIDE)
        col_stat_copy(peer).wait_send()
        copy(pmsg, pstats.at[tslot], psend.at[peer], precv.at[tslot], col_peer(peer)).wait_send()
        return carry

    lax.fori_loop(1, SIDE, sent, 0)

    def terms_sent(n, carry):
        cross_term(n).wait_send()
        for d in range(1, 8):
            z_term(n, d).wait_send()
        return carry

    lax.fori_loop(0, E // WIDE, terms_sent, 0)
    for p in range(len(PIECES)):
        for d in (1, 2, 3):
            slab_copy(p, d).wait_send()
            keep_copy(p, d).wait_send()


def per_device(images, texts, logit_scale):
    f32, bf16 = jnp.float32, jnp.bfloat16
    dma = pltpu.SemaphoreType.DMA
    vmem = pl.BlockSpec(memory_space=pltpu.VMEM)
    smem = pl.BlockSpec(memory_space=pltpu.SMEM)
    loss, image_grad, text_grad = pl.pallas_call(
        kernel,
        out_shape=(
            jax.ShapeDtypeStruct((1,), f32),
            jax.ShapeDtypeStruct((ROWS, E), f32),
            jax.ShapeDtypeStruct((ROWS, E), f32),
        ),
        in_specs=[vmem, vmem, smem],
        out_specs=(smem, vmem, vmem),
        scratch_shapes=[
            pltpu.VMEM((SIDE, ROWS, E), bf16),
            pltpu.VMEM((SIDE, ROWS, E), bf16),
            pltpu.VMEM((TILE, E), bf16),
            pltpu.VMEM((TILE, E), bf16),
            pltpu.VMEM((TILE, TILE), f32),
            pltpu.VMEM((TILE, TILE), f32),
            pltpu.VMEM((TILE, TILE), f32),
            pltpu.VMEM((TILE, TILE), bf16),
            pltpu.VMEM((TILE, TILE), bf16),
            pltpu.VMEM((TILE, 128), f32),
            pltpu.VMEM((8, TILE), f32),
            pltpu.VMEM((8, TILE), f32),
            pltpu.VMEM((8, TILE), f32),
            pltpu.VMEM((TILE, 128), f32),
            pltpu.VMEM((8, WIDE), f32),
            pltpu.VMEM((8, WIDE), f32),
            pltpu.VMEM((SIDE, 8, WIDE), f32),
            pltpu.VMEM((SIDE, 8, WIDE), f32),
            pltpu.VMEM((8, 128), f32),
            pltpu.VMEM((SIDE, 8, 128), f32),
            pltpu.VMEM((8, 128), f32),
            pltpu.VMEM((SIDE, 8, 128), f32),
            pltpu.VMEM((8, ROWS, E), f32),
            pltpu.VMEM((8, ROWS, E), f32),
            pltpu.VMEM((8, ROWS, E), f32),
            pltpu.VMEM((8, ROWS, E), bf16),
            pltpu.VMEM((8, ROWS, E), bf16),
            pltpu.VMEM((SIDE, ROWS, E), f32),
            pltpu.VMEM((2, 4, 4, ROWS, HALF), bf16),
            pltpu.VMEM((2, 4, 4, ROWS, HALF), bf16),
            pltpu.VMEM((2, 4, ROWS, HALF), bf16),
            pltpu.VMEM((2, 4, ROWS, HALF), bf16),
            pltpu.VMEM((ROWS, E), f32),
            dma((2, 4)), dma((8,)), dma((SIDE,)),
            dma((2, 4)), dma((2, SIDE)), dma((2, SIDE)),
            dma((SIDE,)), dma((SIDE,)), dma((SIDE,)), dma((SIDE,)),
            dma((SIDE,)), dma((SIDE,)), dma((SIDE,)), dma((SIDE,)),
            dma((5,)), dma((5,)), dma((5, 8)), dma((5, 8)),
            dma((6, 4)), dma((6, 4)), dma((6, 4)), dma((6, 4)),
        ],
        compiler_params=pltpu.CompilerParams(
            collective_id=0, has_side_effects=True, vmem_limit_bytes=60 * 1024 * 1024
        ),
    )(images, texts, logit_scale)
    return loss, image_grad, text_grad


def solution(mesh):
    in_specs = (P(("img", "txt"), None), P(("txt", "img"), None), P())
    out_specs = (P(), P(("img", "txt"), None), P(("txt", "img"), None))
    return jax.shard_map(
        per_device, mesh=mesh, in_specs=in_specs, out_specs=out_specs, check_vma=False
    )
```

```python
import jax
import jax.numpy as jnp
from jax import lax
from jax.experimental import pallas as pl
from jax.experimental.pallas import tpu as pltpu
from jax.sharding import PartitionSpec as P

MESH = pl.DeviceIdType.MESH
ROWS = 56
PITCH = 64
SIDE = 16
TILE = SIDE * PITCH
CORE = 8 * PITCH
E = 1280
PAIRS = 14336
WIDE = 256
CHUNKS = E // WIDE
HALF = 640
FLOOR = -1e30
PIECES = (
    (0, 0, 256, 0),
    (1, 256, 256, 0),
    (0, 512, 256, 256),
    (1, 768, 256, 256),
    (0, 1024, 128, 512),
    (1, 1152, 128, 512),
)
NEAR = (1, 3, 2)


def device(x, y, z, c):
    return (lax.rem(x, 2) * 2 + c, (y * 8 + z) * 2 + lax.div(x, 2))


def kernel(
    images_ref, texts_ref, scale_ref,
    loss_ref, igrad_ref, tgrad_ref,
    ibuf, tbuf, ibig, tbig, tother, logits, prow, pcol, weights, wother, wturned,
    rsub, csum, cmax, dsum, frow, rmsg, cmsg, rstats, cstats, lmsg, lstats, pmsg, pstats,
    ipart, tpart, zout, zagg, zin, sout, sin, pout, pin, pkeep,
    own_sem, zsend, zrecv, isend, icross, tsend, ta0, ta1, tb0, tb1, tc, xsem,
    small_send, small_recv, zosend, zfirst, zlast, ssend, srecv, psend, precv,
):
    img = lax.axis_index("img")
    txt = lax.axis_index("txt")
    x_lo = lax.div(img, 2)
    c = lax.rem(img, 2)
    x_hi = lax.rem(txt, 2)
    x = x_hi * 2 + x_lo
    y = lax.div(txt, 16)
    z = lax.rem(lax.div(txt, 2), 8)
    oc = 1 - c
    islot = c * 8 + z
    tslot = x * 4 + y

    def x_at(d):
        return lax.rem(x + d, 4)

    def y_at(d):
        return lax.rem(y + d, 4)

    def z_at(d):
        return lax.rem(z + d + 8, 8)

    def row_peer(slot):
        return device(x, y, lax.rem(slot, 8), lax.div(slot, 8))

    def col_peer(slot):
        return device(lax.div(slot, 4), lax.rem(slot, 4), z, c)

    twin = device(x, y, z, oc)

    def copy(src, dst, send, recv, where):
        return pltpu.make_async_remote_copy(
            src_ref=src, dst_ref=dst, send_sem=send, recv_sem=recv,
            device_id=where, device_id_type=MESH,
        )

    def wait_on(ref, sem):
        copy(ref, ref, sem, sem, twin).wait_recv()

    barrier = pltpu.get_barrier_semaphore()

    def greet(k, carry):
        pl.semaphore_signal(barrier, inc=1, device_id=row_peer(lax.rem(islot + k, SIDE)), device_id_type=MESH)
        pl.semaphore_signal(barrier, inc=1, device_id=col_peer(lax.rem(tslot + k, SIDE)), device_id_type=MESH)
        return carry

    lax.fori_loop(1, SIDE, greet, 0)
    own_image = pltpu.make_async_copy(images_ref, ibuf.at[islot], own_sem.at[0])
    own_text = pltpu.make_async_copy(texts_ref, tbuf.at[tslot], own_sem.at[1])
    own_image.start()
    own_text.start()
    ibig[...] = jnp.zeros_like(ibig)
    tbig[...] = jnp.zeros_like(tbig)
    own_image.wait()
    own_text.wait()
    pl.semaphore_wait(barrier, 2 * (SIDE - 1))

    def half_of(buf, slot, half):
        return buf.at[slot, :, pl.ds(half * HALF, HALF)]

    def z_copy(owner, way, half):
        ref = half_of(ibuf, c * 8 + owner, half)
        return copy(ref, ref, zsend.at[0], zrecv.at[half * 8 + owner], device(x, y, z_at(1 if way == 0 else -1), c))

    def z_wait(owner, half):
        wait_on(half_of(ibuf, c * 8 + owner, half), zrecv.at[half * 8 + owner])

    def cross_copy(owner):
        ref = ibuf.at[c * 8 + owner]
        return copy(ref, ref, isend.at[0], icross.at[owner], twin)

    def t_copy(slot, half, sem, where):
        ref = half_of(tbuf, slot, half)
        return copy(ref, ref, tsend.at[0], sem, where)

    def place(buf, big, slot):
        big[pl.ds(pl.multiple_of(slot * PITCH, PITCH), ROWS), :] = buf[slot]

    z_copy(z, 0, 0).start()
    z_copy(z, 1, 0).start()
    for d in NEAR:
        t_copy(tslot, 0, ta0.at[x], device(x_at(d), y, z, c)).start()
        t_copy(tslot, 1, ta1.at[y], device(x, y_at(d), z, c)).start()
    z_copy(z, 0, 1).start()
    z_copy(z, 1, 1).start()
    for d in NEAR:
        t_copy(tslot, 1, tb0.at[x], device(x_at(d), y, z, c)).start()
        t_copy(tslot, 0, tb1.at[0], device(x, y_at(d), z, c)).start()
    cross_copy(z).start()
    place(ibuf, ibig, islot)
    place(tbuf, tbig, tslot)
    weights[...] = jnp.zeros_like(weights)
    rsub[...] = jnp.zeros_like(rsub)

    def z_step(step, half):
        left = z_at(-1 - step)
        right = z_at(1 + step)
        z_wait(left, half)
        if step < 2:
            z_copy(left, 0, half).start()
        else:
            @pl.when(c == 0)
            def _():
                z_copy(left, 0, half).start()
        z_wait(right, half)
        if step < 2:
            z_copy(right, 1, half).start()
        else:
            @pl.when(c == 1)
            def _():
                z_copy(right, 1, half).start()
        if half == 1:
            cross_copy(left).start()
            cross_copy(right).start()
            place(ibuf, ibig, c * 8 + left)
            place(ibuf, ibig, c * 8 + right)

    def t_step(d):
        slot0 = x_at(d) * 4 + y
        slot1 = x * 4 + y_at(d)
        wait_on(half_of(tbuf, slot0, 0), ta0.at[x_at(d)])
        for e in NEAR:
            t_copy(slot0, 0, tc.at[x_at(d)], device(x, y_at(e), z, c)).start()
        wait_on(half_of(tbuf, slot1, 1), ta1.at[y_at(d)])
        for e in NEAR:
            t_copy(slot1, 1, tc.at[x], device(x_at(e), y, z, c)).start()

    z_step(0, 0)
    t_step(1)
    z_step(0, 1)
    t_step(3)
    z_step(1, 0)
    t_step(2)
    z_step(1, 1)
    z_step(2, 0)
    z_step(2, 1)
    far = z_at(4)
    z_wait(far, 0)
    z_wait(far, 1)
    cross_copy(far).start()
    place(ibuf, ibig, c * 8 + far)
    wait_on(tbuf.at[pl.ds(0, 3), :, pl.ds(0, HALF)], tb1.at[0])
    for d in NEAR:
        place(tbuf, tbig, x * 4 + y_at(d))

    def other_image(k, carry):
        wait_on(ibuf.at[oc * 8 + k], icross.at[k])
        place(ibuf, ibig, oc * 8 + k)
        return carry

    lax.fori_loop(0, 8, other_image, 0)

    scale = scale_ref[0]

    def score(tile):
        cols = pl.ds(pl.multiple_of(tile * WIDE, WIDE), WIDE)
        part = lax.dot_general(
            ibig[...], tbig[cols, :], (((1,), (1,)), ((), ())), preferred_element_type=jnp.float32
        )
        pad = lax.bitwise_and(lax.broadcasted_iota(jnp.int32, (1, WIDE), 1), PITCH - 1) >= ROWS
        logits[:, cols] = jnp.where(pad, FLOOR, part * scale)

    score(x)
    for d in NEAR:
        tile = x_at(d)
        wait_on(half_of(tbuf, tile * 4 + y, 1), tb0.at[tile])
        wait_on(tbuf.at[pl.ds(0, 3)], tc.at[tile])
        for e in range(4):
            place(tbuf, tbig, tile * 4 + e)
        score(tile)
    text_swap = copy(tbig, tother, xsem.at[0], xsem.at[1], twin)
    text_swap.start()

    def rows_of(k):
        return pl.ds(pl.multiple_of(k * PITCH, PITCH), ROWS)

    cmax[...] = jnp.full_like(cmax, FLOOR)

    def col_max(k, carry):
        cmax[...] = jnp.maximum(cmax[...], jnp.max(logits[rows_of(k), :].reshape(7, 8, TILE), 0))
        return carry

    lax.fori_loop(0, SIDE, col_max, 0)
    col_top = jnp.max(cmax[...], 0, keepdims=True)
    csum[...] = jnp.zeros_like(csum)

    def exponentials(k, carry):
        part = logits[rows_of(k), :]
        top = jnp.max(part, 1, keepdims=True)
        by_row = jnp.exp(part - top)
        by_col = jnp.exp(part - col_top)
        prow[rows_of(k), :] = by_row
        pcol[rows_of(k), :] = by_col
        total = jnp.sum(by_row, 1, keepdims=True)
        first = lax.broadcasted_iota(jnp.int32, (ROWS, 128), 1) == 0
        rsub[rows_of(k), :] = jnp.where(first, top, total)
        csum[...] += jnp.sum(by_col.reshape(7, 8, TILE), 0)
        return carry

    lax.fori_loop(0, SIDE, exponentials, 0)

    row_stats = jnp.transpose(rsub[...], (1, 0))
    col_total_here = jnp.sum(csum[...], 0, keepdims=True)
    for k in range(4):
        part = slice(k * WIDE, (k + 1) * WIDE)
        rmsg[k:k + 1, :] = row_stats[0:1, part]
        rmsg[4 + k:5 + k, :] = row_stats[1:2, part]
        cmsg[k:k + 1, :] = col_top[:, part]
        cmsg[4 + k:5 + k, :] = col_total_here[:, part]

    def spread(msg, stats, which, mine, peer_of):
        stats[mine] = msg[...]

        def send(k, carry):
            copy(msg, stats.at[mine], small_send.at[which], small_recv.at[which], peer_of(lax.rem(mine + k, SIDE))).start()
            return carry

        lax.fori_loop(1, SIDE, send, 0)

    def collect(stats, which):
        wait_on(stats.at[pl.ds(0, SIDE - 1)], small_recv.at[which])

    spread(rmsg, rstats, 0, islot, row_peer)
    spread(cmsg, cstats, 1, tslot, col_peer)

    def diagonal_slot(k):
        row_block = (x_lo * 2 + lax.div(k, 8)) * 64 + (y * 8 + lax.rem(k, 8)) * 2 + x_hi
        here = jnp.logical_and(lax.rem(row_block, 2) == c, lax.rem(lax.div(row_block, 8), 8) == z)
        slot = (lax.rem(lax.div(row_block, 4), 2) * 2 + lax.rem(lax.div(row_block, 2), 2)) * 4 + lax.div(row_block, 64)
        return here, slot

    def pair_mask(slot):
        row = lax.broadcasted_iota(jnp.int32, (ROWS, 128), 0)
        lane = lax.broadcasted_iota(jnp.int32, (ROWS, 128), 1)
        return lane == row + lax.rem(slot, 2) * PITCH

    def pair_cols(slot):
        return pl.ds(pl.multiple_of(lax.div(slot, 2) * 128, 128), 128)

    dsum[...] = jnp.zeros_like(dsum)

    def diagonal_logits(k, carry):
        here, slot = diagonal_slot(k)

        @pl.when(here)
        def _():
            picked = jnp.where(pair_mask(slot), logits[rows_of(k), pair_cols(slot)], 0.0)
            dsum[...] += jnp.sum(picked.reshape(7, 8, 128), 0)

        return carry

    lax.fori_loop(0, SIDE, diagonal_logits, 0)
    collect(rstats, 0)

    def combine(stats, mine):
        peaks = stats[:, 0:4, :]
        totals = stats[:, 4:8, :]
        peak = jnp.max(peaks, 0)
        total = jnp.sum(totals * jnp.exp(peaks - peak[None]), 0)
        factor = 0.5 * jnp.exp(mine[0:4, :] - peak) / total
        return peak + jnp.log(total), factor

    def line(v):
        return jnp.concatenate([v[k:k + 1, :] for k in range(4)], 1)

    row_lse, row_factor = combine(rstats, rmsg)
    frow[...] = jnp.transpose(jnp.broadcast_to(line(row_factor), (128, TILE)), (1, 0))
    collect(cstats, 1)
    col_lse, col_factor = combine(cstats, cmsg)
    csum[0:1, :] = line(col_factor)

    def weigh(k, carry):
        factor = frow[rows_of(k), :][:, 0:1]
        w = factor * prow[rows_of(k), :] + csum[0:1, :] * pcol[rows_of(k), :]
        weights[rows_of(k), :] = w.astype(jnp.bfloat16)
        here, slot = diagonal_slot(k)

        @pl.when(here)
        def _():
            cols = pair_cols(slot)
            v = frow[rows_of(k), :] * prow[rows_of(k), cols] + csum[0:1, cols] * pcol[rows_of(k), cols]
            v = v - jnp.where(pair_mask(slot), 1.0, 0.0)
            weights[rows_of(k), cols] = v.astype(jnp.bfloat16)

        return carry

    lax.fori_loop(oc * 8, oc * 8 + 8, weigh, 0)
    weight_swap = copy(
        weights.at[pl.ds(pl.multiple_of(oc * CORE, CORE), CORE), :], wother, xsem.at[2], xsem.at[3], twin
    )
    weight_swap.start()
    lax.fori_loop(c * 8, c * 8 + 8, weigh, 0)

    index = lax.broadcasted_iota(jnp.int32, (4, WIDE), 0) * WIDE + lax.broadcasted_iota(jnp.int32, (4, WIDE), 1)
    slot_of = lax.shift_right_logical(index, 6)
    valid = lax.bitwise_and(index, PITCH - 1) < ROWS
    terms = jnp.where(valid & (slot_of == islot), row_lse, 0.0) + jnp.where(valid & (slot_of == tslot), col_lse, 0.0)
    term = jnp.sum(jnp.sum(terms, 0, keepdims=True), 1, keepdims=True)
    diagonal = jnp.sum(jnp.sum(dsum[...], 0, keepdims=True), 1, keepdims=True)
    lmsg[...] = jnp.broadcast_to(term - 2.0 * diagonal, (8, 128))
    spread(lmsg, lstats, 2, islot, row_peer)

    for k in range(TILE // 128):
        wturned[:, k * 128:(k + 1) * 128] = jnp.transpose(weights[k * 128:(k + 1) * 128, :], (1, 0))

    def first_peer(axis, f):
        return device(x, f, z, c) if axis == 0 else device(f, y, z, c)

    def second_peer(axis, s):
        return device(s, y, z, c) if axis == 0 else device(x, s, z, c)

    def slab_copy(p, d):
        axis, _, width, at = PIECES[p]
        me = y if axis == 0 else x
        there = lax.rem(me + d, 4)
        cols = pl.ds(at, width)
        return copy(
            sout.at[axis, there, :, :, cols], sin.at[axis, d - 1, :, :, cols],
            ssend.at[0], srecv.at[p], first_peer(axis, there),
        )

    def text_terms(n):
        low = n * WIDE
        tpart[:, low:low + WIDE] = jnp.dot(wturned[...], ibig[:, low:low + WIDE], preferred_element_type=jnp.float32)
        for p, (axis, col, width, at) in enumerate(PIECES):
            if col // WIDE != n:
                continue
            for m in range(SIDE):
                first, second = (m % 4, m // 4) if axis == 0 else (m // 4, m % 4)
                piece = tpart[m * PITCH:m * PITCH + ROWS, col:col + width]
                sout[axis, first, second, :, at:at + width] = piece.astype(jnp.bfloat16)
            for d in (2, 1, 3):
                slab_copy(p, d).start()

    def keep_copy(p, d):
        axis, _, width, at = PIECES[p]
        me = x if axis == 0 else y
        there = lax.rem(me + d, 4)
        cols = pl.ds(at, width)
        return copy(
            pout.at[axis, there, :, cols], pin.at[axis, d - 1, :, cols],
            psend.at[0], precv.at[p], second_peer(axis, there),
        )

    def text_second(p):
        axis, col, width, at = PIECES[p]
        wait_on(sin.at[axis, pl.ds(0, 3), :, :, pl.ds(at, width)], srecv.at[p])
        me = x if axis == 0 else y
        for d in (2, 1, 3, 0):
            s = lax.rem(me + d, 4)
            m = s * 4 + y if axis == 0 else x * 4 + s
            total = tpart[rows_of(m), col:col + width]
            for e in range(3):
                total = total + sin[axis, e, s, :, at:at + width].astype(jnp.float32)
            if d == 0:
                pkeep[:, col:col + width] = total
            else:
                pout[axis, s, :, at:at + width] = total.astype(jnp.bfloat16)
                keep_copy(p, d).start()

    def text_last(p):
        axis, col, width, at = PIECES[p]
        wait_on(pin.at[axis, pl.ds(0, 3), :, pl.ds(at, width)], precv.at[p])
        total = pkeep[:, col:col + width]
        for d in range(3):
            total = total + pin[axis, d, :, at:at + width].astype(jnp.float32)
        tgrad_ref[:, col:col + width] = total

    def image_send(n, src, slot, low, width, sem, d):
        return copy(
            src, zin.at[slot, :, pl.ds(low, width)], zosend.at[0], sem.at[n], device(x, y, z_at(d), c)
        )

    def image_terms(n):
        low = n * WIDE
        cols = pl.ds(low, WIDE)
        mine = pl.ds(pl.multiple_of(c * CORE, CORE), CORE)
        part = jnp.dot(weights[mine, :], tbig[:, cols], preferred_element_type=jnp.float32)
        ipart[:, cols] = part + jnp.dot(wother[...], tother[:, cols], preferred_element_type=jnp.float32)
        for d in (3, -3, 4, 1, -1):
            zout[z_at(d), :, cols] = ipart[rows_of(z_at(d)), cols].astype(jnp.bfloat16)
        image_send(n, zout.at[z_at(4), :, pl.ds(low, 128)], 2, low, 128, zfirst, 2).start()
        image_send(n, zout.at[z_at(4), :, pl.ds(low + 128, 128)], 2, low + 128, 128, zfirst, -2).start()
        image_send(n, zout.at[z_at(3), :, cols], 0, low, WIDE, zfirst, 1).start()
        image_send(n, zout.at[z_at(-3), :, cols], 1, low, WIDE, zfirst, -1).start()
        image_send(n, zout.at[z_at(1), :, cols], 3, low, WIDE, zlast, 1).start()
        image_send(n, zout.at[z_at(-1), :, cols], 4, low, WIDE, zlast, -1).start()

    def image_second(n):
        low = n * WIDE
        cols = pl.ds(low, WIDE)
        wait_on(zin.at[pl.ds(0, 3), :, cols], zfirst.at[n])
        for way in range(2):
            d = 2 if way == 0 else -2
            total = ipart[rows_of(z_at(d)), cols] + zin[way, :, cols].astype(jnp.float32)
            edge = low + way * 128
            side = total[:, way * 128:way * 128 + 128] + zin[2, :, edge:edge + 128].astype(jnp.float32)
            rest = low + 128 - way * 128
            zagg[way, :, edge:edge + 128] = side.astype(jnp.bfloat16)
            zagg[way, :, rest:rest + 128] = total[:, 128 - way * 128:256 - way * 128].astype(jnp.bfloat16)
            image_send(n, zagg.at[way, :, cols], 5 + way, low, WIDE, zlast, d).start()

    def image_last(n):
        cols = pl.ds(n * WIDE, WIDE)
        wait_on(zin.at[pl.ds(3, 4), :, cols], zlast.at[n])
        total = ipart[rows_of(z), cols]
        for k in range(3, 7):
            total = total + zin[k, :, cols].astype(jnp.float32)
        igrad_ref[:, cols] = total

    text_terms(0)
    text_swap.wait()
    weight_swap.wait()
    image_terms(0)
    text_terms(1)
    image_terms(1)
    image_second(0)
    text_terms(2)
    image_terms(2)
    image_second(1)
    text_second(0)
    text_terms(3)
    image_terms(3)
    image_second(2)
    text_second(1)
    text_terms(4)
    image_terms(4)
    image_second(3)
    text_second(2)
    collect(lstats, 2)
    pmsg[...] = jnp.sum(lstats[...], 0)
    spread(pmsg, pstats, 3, tslot, col_peer)
    image_second(4)
    text_second(3)
    text_second(4)
    text_second(5)
    for n in range(CHUNKS):
        image_last(n)
        text_last(n)
    text_last(5)
    collect(pstats, 3)
    loss_ref[...] = (jnp.sum(pstats[...], 0) / (2.0 * PAIRS))[0:1, 0:1]

    wait_on(ibuf.at[pl.ds(0, 7)], zsend.at[0])
    wait_on(ibuf.at[pl.ds(0, 8)], isend.at[0])
    wait_on(tbuf.at[pl.ds(0, 15)], tsend.at[0])
    wait_on(rstats.at[pl.ds(0, SIDE - 1)], small_send.at[0])
    wait_on(cstats.at[pl.ds(0, SIDE - 1)], small_send.at[1])
    wait_on(lstats.at[pl.ds(0, SIDE - 1)], small_send.at[2])
    wait_on(pstats.at[pl.ds(0, SIDE - 1)], small_send.at[3])
    wait_on(zin, zosend.at[0])
    wait_on(sout.at[:, pl.ds(0, 3)], ssend.at[0])
    wait_on(pout.at[:, pl.ds(0, 3)], psend.at[0])


def per_device(images, texts, logit_scale):
    f32, bf16 = jnp.float32, jnp.bfloat16
    dma = pltpu.SemaphoreType.DMA
    vmem = pl.BlockSpec(memory_space=pltpu.VMEM)
    smem = pl.BlockSpec(memory_space=pltpu.SMEM)
    hbm = pl.BlockSpec(memory_space=pl.ANY)
    loss, image_grad, text_grad = pl.pallas_call(
        kernel,
        out_shape=(
            jax.ShapeDtypeStruct((1, 1), f32),
            jax.ShapeDtypeStruct((ROWS, E), f32),
            jax.ShapeDtypeStruct((ROWS, E), f32),
        ),
        in_specs=[hbm, hbm, smem],
        out_specs=(vmem, vmem, vmem),
        scratch_shapes=[
            pltpu.VMEM((SIDE, ROWS, E), bf16),
            pltpu.VMEM((SIDE, ROWS, E), bf16),
            pltpu.VMEM((TILE, E), bf16),
            pltpu.VMEM((TILE, E), bf16),
            pltpu.VMEM((TILE, E), bf16),
            pltpu.VMEM((TILE, TILE), f32),
            pltpu.VMEM((TILE, TILE), f32),
            pltpu.VMEM((TILE, TILE), f32),
            pltpu.VMEM((TILE, TILE), bf16),
            pltpu.VMEM((CORE, TILE), bf16),
            pltpu.VMEM((TILE, TILE), bf16),
            pltpu.VMEM((TILE, 128), f32),
            pltpu.VMEM((8, TILE), f32),
            pltpu.VMEM((8, TILE), f32),
            pltpu.VMEM((8, 128), f32),
            pltpu.VMEM((TILE, 128), f32),
            pltpu.VMEM((8, WIDE), f32),
            pltpu.VMEM((8, WIDE), f32),
            pltpu.VMEM((SIDE, 8, WIDE), f32),
            pltpu.VMEM((SIDE, 8, WIDE), f32),
            pltpu.VMEM((8, 128), f32),
            pltpu.VMEM((SIDE, 8, 128), f32),
            pltpu.VMEM((8, 128), f32),
            pltpu.VMEM((SIDE, 8, 128), f32),
            pltpu.VMEM((CORE, E), f32),
            pltpu.VMEM((TILE, E), f32),
            pltpu.VMEM((8, ROWS, E), bf16),
            pltpu.VMEM((2, ROWS, E), bf16),
            pltpu.VMEM((7, ROWS, E), bf16),
            pltpu.VMEM((2, 4, 4, ROWS, HALF), bf16),
            pltpu.VMEM((2, 3, 4, ROWS, HALF), bf16),
            pltpu.VMEM((2, 4, ROWS, HALF), bf16),
            pltpu.VMEM((2, 3, ROWS, HALF), bf16),
            pltpu.VMEM((ROWS, E), f32),
            dma((2,)), dma((1,)), dma((16,)), dma((1,)), dma((8,)),
            dma((1,)), dma((4,)), dma((4,)), dma((4,)), dma((1,)), dma((4,)), dma((4,)),
            dma((4,)), dma((4,)), dma((1,)), dma((5,)), dma((5,)),
            dma((1,)), dma((6,)), dma((1,)), dma((6,)),
        ],
        compiler_params=pltpu.CompilerParams(
            collective_id=0, has_side_effects=True, vmem_limit_bytes=60 * 1024 * 1024
        ),
    )(images, texts, logit_scale)
    return loss.reshape(1), image_grad, text_grad


def solution(mesh):
    in_specs = (P(("img", "txt"), None), P(("txt", "img"), None), P())
    out_specs = (P(), P(("img", "txt"), None), P(("txt", "img"), None))
    return jax.shard_map(
        per_device, mesh=mesh, in_specs=in_specs, out_specs=out_specs, check_vma=False
    )
```

```python
import jax
import jax.numpy as jnp
from jax import lax
from jax.experimental import pallas as pl
from jax.experimental.pallas import tpu as pltpu
from jax.sharding import PartitionSpec as P

MESH = pl.DeviceIdType.MESH
ROWS = 56
PITCH = 64
SIDE = 16
TILE = SIDE * PITCH
CORE = 8 * PITCH
E = 1280
PAIRS = 14336
WIDE = 256
CHUNKS = E // WIDE
HALF = 640
FLOOR = -1e30
PIECES = (
    (0, 0, 256, 0),
    (1, 256, 256, 0),
    (0, 512, 256, 256),
    (1, 768, 256, 256),
    (0, 1024, 128, 512),
    (1, 1152, 128, 512),
)
NEAR = (1, 3, 2)


def device(x, y, z, c):
    return (lax.rem(x, 2) * 2 + c, (y * 8 + z) * 2 + lax.div(x, 2))


def kernel(
    images_ref, texts_ref, scale_ref,
    loss_ref, igrad_ref, tgrad_ref,
    ibuf, tbuf, ibig, tbig, tother, logits, prow, pcol, weights, wother, wturned,
    rsub, csum, cmax, cpeak, cfac, dsum, frow, rmsg, cmsg, rstats, cstats, lmsg, lstats, pmsg, pstats,
    ipart, tpart, zout, zagg, zin, sout, sin, pout, pin, pkeep,
    own_sem, zsend, zrecv, isend, icross, tsend, tfirst, tplus, tminus, tfar, xsem,
    small_send, small_recv, zosend, zfirst, zlast, ssend, srecv, psend, precv,
):
    img = lax.axis_index("img")
    txt = lax.axis_index("txt")
    x_lo = lax.div(img, 2)
    c = lax.rem(img, 2)
    x_hi = lax.rem(txt, 2)
    x = x_hi * 2 + x_lo
    y = lax.div(txt, 16)
    z = lax.rem(lax.div(txt, 2), 8)
    oc = 1 - c
    islot = c * 8 + z
    tslot = x * 4 + y

    def x_at(d):
        return lax.rem(x + d, 4)

    def y_at(d):
        return lax.rem(y + d, 4)

    def z_at(d):
        return lax.rem(z + d + 8, 8)

    def row_peer(slot):
        return device(x, y, lax.rem(slot, 8), lax.div(slot, 8))

    def col_peer(slot):
        return device(lax.div(slot, 4), lax.rem(slot, 4), z, c)

    twin = device(x, y, z, oc)

    def copy(src, dst, send, recv, where):
        return pltpu.make_async_remote_copy(
            src_ref=src, dst_ref=dst, send_sem=send, recv_sem=recv,
            device_id=where, device_id_type=MESH,
        )

    def wait_on(ref, sem):
        copy(ref, ref, sem, sem, twin).wait_recv()

    barrier = pltpu.get_barrier_semaphore()

    def greet(k, carry):
        pl.semaphore_signal(barrier, inc=1, device_id=row_peer(lax.rem(islot + k, SIDE)), device_id_type=MESH)
        pl.semaphore_signal(barrier, inc=1, device_id=col_peer(lax.rem(tslot + k, SIDE)), device_id_type=MESH)
        return carry

    lax.fori_loop(1, SIDE, greet, 0)
    own_image = pltpu.make_async_copy(images_ref, ibuf.at[islot], own_sem.at[0])
    own_text = pltpu.make_async_copy(texts_ref, tbuf.at[tslot], own_sem.at[1])
    own_image.start()
    own_text.start()
    ibig[...] = jnp.zeros_like(ibig)
    tbig[...] = jnp.zeros_like(tbig)
    own_image.wait()
    own_text.wait()
    pl.semaphore_wait(barrier, 2 * (SIDE - 1))

    def half_of(buf, slot, half):
        return buf.at[slot, :, pl.ds(half * HALF, HALF)]

    def z_copy(owner, way, half):
        ref = half_of(ibuf, c * 8 + owner, half)
        return copy(ref, ref, zsend.at[0], zrecv.at[half * 8 + owner], device(x, y, z_at(1 if way == 0 else -1), c))

    def z_wait(owner, half):
        wait_on(half_of(ibuf, c * 8 + owner, half), zrecv.at[half * 8 + owner])

    def cross_copy(owner):
        ref = ibuf.at[c * 8 + owner]
        return copy(ref, ref, isend.at[0], icross.at[owner], twin)

    def t_slot(half, u, v):
        return u * 4 + v if half == 0 else v * 4 + u

    def t_here(half):
        return (x, y) if half == 0 else (y, x)

    def t_device(half, u, v):
        return device(u, v, z, c) if half == 0 else device(v, u, z, c)

    def t_send(half, u, v, sem, to_u, to_v):
        ref = half_of(tbuf, t_slot(half, u, v), half)
        copy(ref, ref, tsend.at[0], sem.at[half * 4 + u], t_device(half, to_u, to_v)).start()

    def t_wait(half, u, v, sem):
        wait_on(half_of(tbuf, t_slot(half, u, v), half), sem.at[half * 4 + u])

    def t_first(half):
        u, v = t_here(half)
        for d in NEAR:
            t_send(half, u, v, tfirst, lax.rem(u + d, 4), v)

    def t_second(half, d):
        u, v = t_here(half)
        there = lax.rem(u + d, 4)
        if d:
            t_wait(half, there, v, tfirst)
        t_send(half, there, v, tplus, u, lax.rem(v + 1, 4))
        t_send(half, there, v, tminus, u, lax.rem(v + 3, 4))

    def t_pass(half, d):
        u, v = t_here(half)
        there = lax.rem(u + d, 4)
        before = lax.rem(v + 3, 4)
        after = lax.rem(v + 1, 4)
        t_wait(half, there, before, tplus)
        if d < 2:
            t_send(half, there, before, tfar, u, after)
        t_wait(half, there, after, tminus)
        if d >= 2:
            t_send(half, there, after, tfar, u, before)

    def t_last(half, d):
        u, v = t_here(half)
        t_wait(half, lax.rem(u + d, 4), lax.rem(v + 2, 4), tfar)

    def place(buf, big, slot):
        big[pl.ds(pl.multiple_of(slot * PITCH, PITCH), ROWS), :] = buf[slot]

    t_first(0)
    t_first(1)
    z_copy(z, 0, 0).start()
    z_copy(z, 1, 0).start()
    t_second(0, 0)
    t_second(1, 0)
    z_copy(z, 0, 1).start()
    z_copy(z, 1, 1).start()
    cross_copy(z).start()
    place(ibuf, ibig, islot)
    place(tbuf, tbig, tslot)
    weights[...] = jnp.zeros_like(weights)
    rsub[...] = jnp.zeros_like(rsub)

    def z_step(step, half):
        left = z_at(-1 - step)
        right = z_at(1 + step)
        z_wait(left, half)
        if step < 2:
            z_copy(left, 0, half).start()
        else:
            @pl.when(c == 0)
            def _():
                z_copy(left, 0, half).start()
        z_wait(right, half)
        if step < 2:
            z_copy(right, 1, half).start()
        else:
            @pl.when(c == 1)
            def _():
                z_copy(right, 1, half).start()
        if half == 1:
            cross_copy(left).start()
            cross_copy(right).start()
            place(ibuf, ibig, c * 8 + left)
            place(ibuf, ibig, c * 8 + right)

    def t_both(what, d):
        what(0, d)
        what(1, d)

    z_step(0, 0)
    t_both(t_second, 1)
    z_step(0, 1)
    t_both(t_second, 3)
    t_both(t_pass, 0)
    z_step(1, 0)
    t_both(t_second, 2)
    t_both(t_pass, 1)
    z_step(1, 1)
    t_both(t_pass, 3)
    z_step(2, 0)
    t_both(t_pass, 2)
    z_step(2, 1)
    far = z_at(4)
    z_wait(far, 0)
    z_wait(far, 1)
    cross_copy(far).start()
    place(ibuf, ibig, c * 8 + far)
    def other_image(k, carry):
        wait_on(ibuf.at[oc * 8 + k], icross.at[k])
        place(ibuf, ibig, oc * 8 + k)
        return carry

    lax.fori_loop(0, 8, other_image, 0)

    scale = scale_ref[0]

    def score(tile):
        cols = pl.ds(pl.multiple_of(tile * WIDE, WIDE), WIDE)
        part = lax.dot_general(
            ibig[...], tbig[cols, :], (((1,), (1,)), ((), ())), preferred_element_type=jnp.float32
        )
        pad = lax.bitwise_and(lax.broadcasted_iota(jnp.int32, (1, WIDE), 1), PITCH - 1) >= ROWS
        logits[:, cols] = jnp.where(pad, FLOOR, part * scale)

    def rows_of(k):
        return pl.ds(pl.multiple_of(k * PITCH, PITCH), ROWS)

    def tile_cols(d):
        return pl.ds(pl.multiple_of(x_at(d) * WIDE, WIDE), WIDE)

    def swap_texts(d):
        rows = tile_cols(d)
        return copy(tbig.at[rows, :], tother.at[rows, :], xsem.at[0], xsem.at[1], twin)

    def exponentials(d):
        cols = tile_cols(d)
        cmax[...] = jnp.full_like(cmax, FLOOR)

        def col_max(k, carry):
            cmax[...] = jnp.maximum(cmax[...], jnp.max(logits[rows_of(k), cols].reshape(7, 8, WIDE), 0))
            return carry

        lax.fori_loop(0, SIDE, col_max, 0)
        top = jnp.max(cmax[...], 0, keepdims=True)
        cpeak[0:1, cols] = top
        csum[:, cols] = jnp.zeros((8, WIDE), jnp.float32)

        def one(k, carry):
            part = logits[rows_of(k), cols]
            peak = jnp.max(part, 1, keepdims=True)
            by_row = jnp.exp(part - peak)
            by_col = jnp.exp(part - top)
            prow[rows_of(k), cols] = by_row
            pcol[rows_of(k), cols] = by_col
            total = jnp.sum(by_row, 1, keepdims=True)
            at = lax.broadcasted_iota(jnp.int32, (ROWS, 128), 1)
            rsub[rows_of(k), :] = jnp.where(at == 2 * d, peak, jnp.where(at == 2 * d + 1, total, rsub[rows_of(k), :]))
            csum[:, cols] += jnp.sum(by_col.reshape(7, 8, WIDE), 0)
            return carry

        lax.fori_loop(0, SIDE, one, 0)

    for d in (0, 1, 3, 2):
        t_last(0, d)
        if d == 2:
            for e in range(4):
                t_last(1, e)
        for e in range(1 if d == 0 else 0, 4):
            place(tbuf, tbig, x_at(d) * 4 + y_at(e))
        swap_texts(d).start()
        score(x_at(d))
        exponentials(d)

    row_stats = jnp.transpose(rsub[...], (1, 0))

    def fold(v):
        return jnp.concatenate([v[:, k * WIDE:(k + 1) * WIDE] for k in range(4)], 0)

    def line(v):
        return jnp.concatenate([v[k:k + 1, :] for k in range(4)], 1)

    tile_peaks = [fold(row_stats[2 * d:2 * d + 1, :]) for d in range(4)]
    tile_totals = [fold(row_stats[2 * d + 1:2 * d + 2, :]) for d in range(4)]
    row_top = jnp.maximum(jnp.maximum(tile_peaks[0], tile_peaks[1]), jnp.maximum(tile_peaks[2], tile_peaks[3]))
    row_total = jnp.zeros_like(row_top)
    for d in range(4):
        row_total = row_total + tile_totals[d] * jnp.exp(tile_peaks[d] - row_top)
    rmsg[0:4, :] = row_top
    rmsg[4:8, :] = row_total
    cmsg[0:4, :] = fold(cpeak[0:1, :])
    cmsg[4:8, :] = fold(jnp.sum(csum[...], 0, keepdims=True))

    def spread(msg, stats, which, mine, peer_of):
        stats[mine] = msg[...]

        def send(k, carry):
            copy(msg, stats.at[mine], small_send.at[which], small_recv.at[which], peer_of(lax.rem(mine + k, SIDE))).start()
            return carry

        lax.fori_loop(1, SIDE, send, 0)

    def collect(stats, which):
        wait_on(stats.at[pl.ds(0, SIDE - 1)], small_recv.at[which])

    spread(rmsg, rstats, 0, islot, row_peer)
    spread(cmsg, cstats, 1, tslot, col_peer)

    def diagonal_slot(k):
        row_block = (x_lo * 2 + lax.div(k, 8)) * 64 + (y * 8 + lax.rem(k, 8)) * 2 + x_hi
        here = jnp.logical_and(lax.rem(row_block, 2) == c, lax.rem(lax.div(row_block, 8), 8) == z)
        slot = (lax.rem(lax.div(row_block, 4), 2) * 2 + lax.rem(lax.div(row_block, 2), 2)) * 4 + lax.div(row_block, 64)
        return here, slot

    def pair_mask(slot):
        row = lax.broadcasted_iota(jnp.int32, (ROWS, 128), 0)
        lane = lax.broadcasted_iota(jnp.int32, (ROWS, 128), 1)
        return lane == row + lax.rem(slot, 2) * PITCH

    def pair_cols(slot):
        return pl.ds(pl.multiple_of(lax.div(slot, 2) * 128, 128), 128)

    dsum[...] = jnp.zeros_like(dsum)

    def diagonal_logits(k, carry):
        here, slot = diagonal_slot(k)

        @pl.when(here)
        def _():
            picked = jnp.where(pair_mask(slot), logits[rows_of(k), pair_cols(slot)], 0.0)
            dsum[...] += jnp.sum(picked.reshape(7, 8, 128), 0)

        return carry

    lax.fori_loop(0, SIDE, diagonal_logits, 0)
    collect(rstats, 0)

    def combine(stats):
        peaks = stats[:, 0:4, :]
        totals = stats[:, 4:8, :]
        peak = jnp.max(peaks, 0)
        total = jnp.sum(totals * jnp.exp(peaks - peak[None]), 0)
        return peak, total

    row_peak, row_total = combine(rstats)
    factors = [line(0.5 * jnp.exp(tile_peaks[d] - row_peak) / row_total) for d in range(4)]
    frow[...] = jnp.transpose(jnp.concatenate(factors + [jnp.zeros((124, TILE), jnp.float32)], 0), (1, 0))
    row_lse = row_peak + jnp.log(row_total)
    collect(cstats, 1)
    col_peak, col_total = combine(cstats)
    cfac[0:1, :] = line(0.5 * jnp.exp(cmsg[0:4, :] - col_peak) / col_total)
    col_lse = col_peak + jnp.log(col_total)

    def weigh(k, carry):
        rows = rows_of(k)
        for d in range(4):
            cols = tile_cols(d)
            w = frow[rows, d:d + 1] * prow[rows, cols] + cfac[0:1, cols] * pcol[rows, cols]
            weights[rows, cols] = w.astype(jnp.bfloat16)
        here, slot = diagonal_slot(k)

        @pl.when(here)
        def _():
            cols = pair_cols(slot)
            lane = lax.broadcasted_iota(jnp.int32, (ROWS, 128), 1)
            at = lax.rem(lax.div(slot, 4) - x + 4, 4)
            factor = jnp.sum(jnp.where(lane == at, frow[rows, :], 0.0), 1, keepdims=True)
            v = factor * prow[rows, cols] + cfac[0:1, cols] * pcol[rows, cols]
            v = v - jnp.where(pair_mask(slot), 1.0, 0.0)
            weights[rows, cols] = v.astype(jnp.bfloat16)

        return carry

    lax.fori_loop(oc * 8, oc * 8 + 8, weigh, 0)
    weight_swap = copy(
        weights.at[pl.ds(pl.multiple_of(oc * CORE, CORE), CORE), :], wother, xsem.at[2], xsem.at[3], twin
    )
    weight_swap.start()
    lax.fori_loop(c * 8, c * 8 + 8, weigh, 0)

    index = lax.broadcasted_iota(jnp.int32, (4, WIDE), 0) * WIDE + lax.broadcasted_iota(jnp.int32, (4, WIDE), 1)
    slot_of = lax.shift_right_logical(index, 6)
    valid = lax.bitwise_and(index, PITCH - 1) < ROWS
    terms = jnp.where(valid & (slot_of == islot), row_lse, 0.0) + jnp.where(valid & (slot_of == tslot), col_lse, 0.0)
    term = jnp.sum(jnp.sum(terms, 0, keepdims=True), 1, keepdims=True)
    diagonal = jnp.sum(jnp.sum(dsum[...], 0, keepdims=True), 1, keepdims=True)
    lmsg[...] = jnp.broadcast_to(term - 2.0 * diagonal, (8, 128))
    spread(lmsg, lstats, 2, islot, row_peer)

    for k in range(TILE // 128):
        wturned[:, k * 128:(k + 1) * 128] = jnp.transpose(weights[k * 128:(k + 1) * 128, :], (1, 0))

    def first_peer(axis, f):
        return device(x, f, z, c) if axis == 0 else device(f, y, z, c)

    def second_peer(axis, s):
        return device(s, y, z, c) if axis == 0 else device(x, s, z, c)

    def slab_copy(p, d):
        axis, _, width, at = PIECES[p]
        me = y if axis == 0 else x
        there = lax.rem(me + d, 4)
        cols = pl.ds(at, width)
        return copy(
            sout.at[axis, there, :, :, cols], sin.at[axis, d - 1, :, :, cols],
            ssend.at[0], srecv.at[p], first_peer(axis, there),
        )

    def text_terms(n):
        low = n * WIDE
        tpart[:, low:low + WIDE] = jnp.dot(wturned[...], ibig[:, low:low + WIDE], preferred_element_type=jnp.float32)
        for p, (axis, col, width, at) in enumerate(PIECES):
            if col // WIDE != n:
                continue
            for m in range(SIDE):
                first, second = (m % 4, m // 4) if axis == 0 else (m // 4, m % 4)
                piece = tpart[m * PITCH:m * PITCH + ROWS, col:col + width]
                sout[axis, first, second, :, at:at + width] = piece.astype(jnp.bfloat16)
            for d in (2, 1, 3):
                slab_copy(p, d).start()

    def keep_copy(p, d):
        axis, _, width, at = PIECES[p]
        me = x if axis == 0 else y
        there = lax.rem(me + d, 4)
        cols = pl.ds(at, width)
        return copy(
            pout.at[axis, there, :, cols], pin.at[axis, d - 1, :, cols],
            psend.at[0], precv.at[p], second_peer(axis, there),
        )

    def text_second(p):
        axis, col, width, at = PIECES[p]
        wait_on(sin.at[axis, pl.ds(0, 3), :, :, pl.ds(at, width)], srecv.at[p])
        me = x if axis == 0 else y
        for d in (2, 1, 3, 0):
            s = lax.rem(me + d, 4)
            m = s * 4 + y if axis == 0 else x * 4 + s
            total = tpart[rows_of(m), col:col + width]
            for e in range(3):
                total = total + sin[axis, e, s, :, at:at + width].astype(jnp.float32)
            if d == 0:
                pkeep[:, col:col + width] = total
            else:
                pout[axis, s, :, at:at + width] = total.astype(jnp.bfloat16)
                keep_copy(p, d).start()

    def text_last(p):
        axis, col, width, at = PIECES[p]
        wait_on(pin.at[axis, pl.ds(0, 3), :, pl.ds(at, width)], precv.at[p])
        total = pkeep[:, col:col + width]
        for d in range(3):
            total = total + pin[axis, d, :, at:at + width].astype(jnp.float32)
        tgrad_ref[:, col:col + width] = total

    def image_send(n, src, slot, low, width, sem, d):
        return copy(
            src, zin.at[slot, :, pl.ds(low, width)], zosend.at[0], sem.at[n], device(x, y, z_at(d), c)
        )

    def image_terms(n):
        low = n * WIDE
        cols = pl.ds(low, WIDE)
        mine = pl.ds(pl.multiple_of(c * CORE, CORE), CORE)
        part = jnp.dot(weights[mine, :], tbig[:, cols], preferred_element_type=jnp.float32)
        ipart[:, cols] = part + jnp.dot(wother[...], tother[:, cols], preferred_element_type=jnp.float32)
        for d in (3, -3, 4, 1, -1):
            zout[z_at(d), :, cols] = ipart[rows_of(z_at(d)), cols].astype(jnp.bfloat16)
        image_send(n, zout.at[z_at(4), :, pl.ds(low, 128)], 2, low, 128, zfirst, 2).start()
        image_send(n, zout.at[z_at(4), :, pl.ds(low + 128, 128)], 2, low + 128, 128, zfirst, -2).start()
        image_send(n, zout.at[z_at(3), :, cols], 0, low, WIDE, zfirst, 1).start()
        image_send(n, zout.at[z_at(-3), :, cols], 1, low, WIDE, zfirst, -1).start()
        image_send(n, zout.at[z_at(1), :, cols], 3, low, WIDE, zlast, 1).start()
        image_send(n, zout.at[z_at(-1), :, cols], 4, low, WIDE, zlast, -1).start()

    def image_second(n):
        low = n * WIDE
        cols = pl.ds(low, WIDE)
        wait_on(zin.at[pl.ds(0, 3), :, cols], zfirst.at[n])
        for way in range(2):
            d = 2 if way == 0 else -2
            total = ipart[rows_of(z_at(d)), cols] + zin[way, :, cols].astype(jnp.float32)
            edge = low + way * 128
            side = total[:, way * 128:way * 128 + 128] + zin[2, :, edge:edge + 128].astype(jnp.float32)
            rest = low + 128 - way * 128
            zagg[way, :, edge:edge + 128] = side.astype(jnp.bfloat16)
            zagg[way, :, rest:rest + 128] = total[:, 128 - way * 128:256 - way * 128].astype(jnp.bfloat16)
            image_send(n, zagg.at[way, :, cols], 5 + way, low, WIDE, zlast, d).start()

    def image_last(n):
        cols = pl.ds(n * WIDE, WIDE)
        wait_on(zin.at[pl.ds(3, 4), :, cols], zlast.at[n])
        total = ipart[rows_of(z), cols]
        for k in range(3, 7):
            total = total + zin[k, :, cols].astype(jnp.float32)
        igrad_ref[:, cols] = total

    text_terms(0)
    wait_on(tother, xsem.at[1])
    weight_swap.wait()
    image_terms(0)
    text_terms(1)
    image_terms(1)
    image_second(0)
    text_terms(2)
    image_terms(2)
    image_second(1)
    text_second(0)
    text_terms(3)
    image_terms(3)
    image_second(2)
    text_second(1)
    text_terms(4)
    image_terms(4)
    image_second(3)
    text_second(2)
    collect(lstats, 2)
    pmsg[...] = jnp.sum(lstats[...], 0)
    spread(pmsg, pstats, 3, tslot, col_peer)
    image_second(4)
    text_second(3)
    text_second(4)
    text_second(5)
    for n in range(CHUNKS):
        image_last(n)
        text_last(n)
    text_last(5)
    collect(pstats, 3)
    loss_ref[...] = (jnp.sum(pstats[...], 0) / (2.0 * PAIRS))[0:1, 0:1]

    wait_on(ibuf.at[pl.ds(0, 7)], zsend.at[0])
    wait_on(ibuf.at[pl.ds(0, 8)], isend.at[0])
    wait_on(tbuf.at[pl.ds(0, 15)], tsend.at[0])
    wait_on(rstats.at[pl.ds(0, SIDE - 1)], small_send.at[0])
    wait_on(cstats.at[pl.ds(0, SIDE - 1)], small_send.at[1])
    wait_on(lstats.at[pl.ds(0, SIDE - 1)], small_send.at[2])
    wait_on(pstats.at[pl.ds(0, SIDE - 1)], small_send.at[3])
    wait_on(tbig, xsem.at[0])
    wait_on(zin, zosend.at[0])
    wait_on(sout.at[:, pl.ds(0, 3)], ssend.at[0])
    wait_on(pout.at[:, pl.ds(0, 3)], psend.at[0])


def per_device(images, texts, logit_scale):
    f32, bf16 = jnp.float32, jnp.bfloat16
    dma = pltpu.SemaphoreType.DMA
    vmem = pl.BlockSpec(memory_space=pltpu.VMEM)
    smem = pl.BlockSpec(memory_space=pltpu.SMEM)
    hbm = pl.BlockSpec(memory_space=pl.ANY)
    loss, image_grad, text_grad = pl.pallas_call(
        kernel,
        out_shape=(
            jax.ShapeDtypeStruct((1, 1), f32),
            jax.ShapeDtypeStruct((ROWS, E), f32),
            jax.ShapeDtypeStruct((ROWS, E), f32),
        ),
        in_specs=[hbm, hbm, smem],
        out_specs=(vmem, vmem, vmem),
        scratch_shapes=[
            pltpu.VMEM((SIDE, ROWS, E), bf16),
            pltpu.VMEM((SIDE, ROWS, E), bf16),
            pltpu.VMEM((TILE, E), bf16),
            pltpu.VMEM((TILE, E), bf16),
            pltpu.VMEM((TILE, E), bf16),
            pltpu.VMEM((TILE, TILE), f32),
            pltpu.VMEM((TILE, TILE), f32),
            pltpu.VMEM((TILE, TILE), f32),
            pltpu.VMEM((TILE, TILE), bf16),
            pltpu.VMEM((CORE, TILE), bf16),
            pltpu.VMEM((TILE, TILE), bf16),
            pltpu.VMEM((TILE, 128), f32),
            pltpu.VMEM((8, TILE), f32),
            pltpu.VMEM((8, WIDE), f32),
            pltpu.VMEM((8, TILE), f32),
            pltpu.VMEM((8, TILE), f32),
            pltpu.VMEM((8, 128), f32),
            pltpu.VMEM((TILE, 128), f32),
            pltpu.VMEM((8, WIDE), f32),
            pltpu.VMEM((8, WIDE), f32),
            pltpu.VMEM((SIDE, 8, WIDE), f32),
            pltpu.VMEM((SIDE, 8, WIDE), f32),
            pltpu.VMEM((8, 128), f32),
            pltpu.VMEM((SIDE, 8, 128), f32),
            pltpu.VMEM((8, 128), f32),
            pltpu.VMEM((SIDE, 8, 128), f32),
            pltpu.VMEM((CORE, E), f32),
            pltpu.VMEM((TILE, E), f32),
            pltpu.VMEM((8, ROWS, E), bf16),
            pltpu.VMEM((2, ROWS, E), bf16),
            pltpu.VMEM((7, ROWS, E), bf16),
            pltpu.VMEM((2, 4, 4, ROWS, HALF), bf16),
            pltpu.VMEM((2, 3, 4, ROWS, HALF), bf16),
            pltpu.VMEM((2, 4, ROWS, HALF), bf16),
            pltpu.VMEM((2, 3, ROWS, HALF), bf16),
            pltpu.VMEM((ROWS, E), f32),
            dma((2,)), dma((1,)), dma((16,)), dma((1,)), dma((8,)),
            dma((1,)), dma((8,)), dma((8,)), dma((8,)), dma((8,)), dma((4,)),
            dma((4,)), dma((4,)), dma((1,)), dma((5,)), dma((5,)),
            dma((1,)), dma((6,)), dma((1,)), dma((6,)),
        ],
        compiler_params=pltpu.CompilerParams(
            collective_id=0, has_side_effects=True, vmem_limit_bytes=60 * 1024 * 1024
        ),
    )(images, texts, logit_scale)
    return loss.reshape(1), image_grad, text_grad


def solution(mesh):
    in_specs = (P(("img", "txt"), None), P(("txt", "img"), None), P())
    out_specs = (P(), P(("img", "txt"), None), P(("txt", "img"), None))
    return jax.shard_map(
        per_device, mesh=mesh, in_specs=in_specs, out_specs=out_specs, check_vma=False
    )
```

```python
import jax
import jax.numpy as jnp
from jax import lax
from jax.experimental import pallas as pl
from jax.experimental.pallas import tpu as pltpu
from jax.sharding import PartitionSpec as P

MESH = pl.DeviceIdType.MESH
ROWS = 56
PITCH = 64
SIDE = 16
TILE = SIDE * PITCH
CORE = 8 * PITCH
E = 1280
PAIRS = 14336
WIDE = 256
CHUNKS = E // WIDE
HALF = 640
FLOOR = -1e30
PIECES = (
    (0, 0, 256, 0),
    (1, 256, 256, 0),
    (0, 512, 256, 256),
    (1, 768, 256, 256),
    (0, 1024, 128, 512),
    (1, 1152, 128, 512),
)
NEAR = (1, 3, 2)


def device(x, y, z, c):
    return (lax.rem(x, 2) * 2 + c, (y * 8 + z) * 2 + lax.div(x, 2))


def kernel(
    images_ref, texts_ref, scale_ref,
    loss_ref, igrad_ref, tgrad_ref,
    stage, ibig, tbig, tother, logits, prow, pcol, weights, wother, wturned,
    rsub, csum, cmax, dsum, frow, rmsg, cmsg, rstats, cstats, lmsg, lstats, pmsg, pstats,
    ipart, tpart, zout, zagg, zin, sout, sin, pout, pin, pkeep,
    own_sem, zsend, zrecv, isend, icross, tsend, tfirst, tplus, tminus, tfar, xsem,
    small_send, small_recv, zosend, zfirst, zlast, ssend, srecv, psend, precv,
):
    img = lax.axis_index("img")
    txt = lax.axis_index("txt")
    x_lo = lax.div(img, 2)
    c = lax.rem(img, 2)
    x_hi = lax.rem(txt, 2)
    x = x_hi * 2 + x_lo
    y = lax.div(txt, 16)
    z = lax.rem(lax.div(txt, 2), 8)
    oc = 1 - c
    islot = c * 8 + z
    tslot = x * 4 + y

    def x_at(d):
        return lax.rem(x + d, 4)

    def y_at(d):
        return lax.rem(y + d, 4)

    def z_at(d):
        return lax.rem(z + d + 8, 8)

    def row_peer(slot):
        return device(x, y, lax.rem(slot, 8), lax.div(slot, 8))

    def col_peer(slot):
        return device(lax.div(slot, 4), lax.rem(slot, 4), z, c)

    twin = device(x, y, z, oc)

    def copy(src, dst, send, recv, where):
        return pltpu.make_async_remote_copy(
            src_ref=src, dst_ref=dst, send_sem=send, recv_sem=recv,
            device_id=where, device_id_type=MESH,
        )

    def wait_on(ref, sem):
        copy(ref, ref, sem, sem, twin).wait_recv()

    barrier = pltpu.get_barrier_semaphore()

    def greet(k, carry):
        pl.semaphore_signal(barrier, inc=1, device_id=row_peer(lax.rem(islot + k, SIDE)), device_id_type=MESH)
        pl.semaphore_signal(barrier, inc=1, device_id=col_peer(lax.rem(tslot + k, SIDE)), device_id_type=MESH)
        return carry

    lax.fori_loop(1, SIDE, greet, 0)
    own_image = pltpu.make_async_copy(images_ref, stage.at[0], own_sem.at[0])
    own_text = pltpu.make_async_copy(texts_ref, stage.at[1], own_sem.at[1])
    own_image.start()
    own_text.start()

    def block_rows(slot):
        return pl.ds(pl.multiple_of(slot * PITCH, PITCH), PITCH)

    ibig[block_rows(islot), :] = jnp.zeros((PITCH, E), jnp.bfloat16)
    tbig[block_rows(tslot), :] = jnp.zeros((PITCH, E), jnp.bfloat16)
    own_image.wait()
    own_text.wait()
    ibig[pl.ds(pl.multiple_of(islot * PITCH, PITCH), ROWS), :] = stage[0]
    tbig[pl.ds(pl.multiple_of(tslot * PITCH, PITCH), ROWS), :] = stage[1]
    pl.semaphore_wait(barrier, 2 * (SIDE - 1))

    def half_of(big, slot, half):
        return big.at[block_rows(slot), pl.ds(half * HALF, HALF)]

    def z_copy(owner, way, half, far=False):
        ref = half_of(ibig, c * 8 + owner, half)
        d = 2 if far else 1
        return copy(ref, ref, zsend.at[0], zrecv.at[half * 8 + owner], device(x, y, z_at(d if way == 0 else -d), c))

    def z_wait(owner, half):
        wait_on(half_of(ibig, c * 8 + owner, half), zrecv.at[half * 8 + owner])

    def cross_copy(owner, half):
        ref = half_of(ibig, c * 8 + owner, half)
        copy(ref, ref, isend.at[0], icross.at[half * 8 + owner], twin).start()

    def t_slot(half, u, v):
        return u * 4 + v if half == 0 else v * 4 + u

    def t_here(half):
        return (x, y) if half == 0 else (y, x)

    def t_device(half, u, v):
        return device(u, v, z, c) if half == 0 else device(v, u, z, c)

    def t_send(half, u, v, sem, to_u, to_v):
        ref = half_of(tbig, t_slot(half, u, v), half)
        copy(ref, ref, tsend.at[0], sem.at[half * 4 + u], t_device(half, to_u, to_v)).start()

    def t_wait(half, u, v, sem):
        wait_on(half_of(tbig, t_slot(half, u, v), half), sem.at[half * 4 + u])

    def t_first(half):
        u, v = t_here(half)
        for d in NEAR:
            t_send(half, u, v, tfirst, lax.rem(u + d, 4), v)

    def t_second(half, d):
        u, v = t_here(half)
        there = lax.rem(u + d, 4)
        if d:
            t_wait(half, there, v, tfirst)
        t_send(half, there, v, tplus, u, lax.rem(v + 1, 4))
        t_send(half, there, v, tminus, u, lax.rem(v + 3, 4))

    def t_pass(half, d):
        u, v = t_here(half)
        there = lax.rem(u + d, 4)
        before = lax.rem(v + 3, 4)
        after = lax.rem(v + 1, 4)
        t_wait(half, there, before, tplus)
        if d < 2:
            t_send(half, there, before, tfar, u, after)
        t_wait(half, there, after, tminus)
        if d >= 2:
            t_send(half, there, after, tfar, u, before)

    def t_last(half, d):
        u, v = t_here(half)
        t_wait(half, lax.rem(u + d, 4), lax.rem(v + 2, 4), tfar)

    t_first(0)
    t_first(1)
    z_copy(z, 0, 0).start()
    z_copy(z, 1, 0).start()
    t_second(0, 0)
    t_second(1, 0)
    z_copy(z, 0, 1).start()
    z_copy(z, 1, 1).start()
    cross_copy(z, 0)
    cross_copy(z, 1)
    weights[...] = jnp.zeros_like(weights)
    rsub[...] = jnp.zeros_like(rsub)

    def z_step(step, half):
        left = z_at(-1 - step)
        right = z_at(1 + step)
        z_wait(left, half)
        if step < 2:
            z_copy(left, 0, half).start()
        if step == 1:
            @pl.when(c == 0)
            def _():
                z_copy(left, 0, half, True).start()
        cross_copy(left, half)
        z_wait(right, half)
        if step < 2:
            z_copy(right, 1, half).start()
        if step == 1:
            @pl.when(c == 1)
            def _():
                z_copy(right, 1, half, True).start()
        cross_copy(right, half)

    def t_both(what, d):
        what(0, d)
        what(1, d)

    z_step(0, 0)
    t_both(t_second, 1)
    z_step(0, 1)
    t_both(t_second, 3)
    t_both(t_pass, 0)
    z_step(1, 0)
    t_both(t_second, 2)
    t_both(t_pass, 1)
    z_step(1, 1)
    t_both(t_pass, 3)
    z_step(2, 0)
    t_both(t_pass, 2)
    z_step(2, 1)
    for half in range(2):
        z_wait(z_at(4), half)
        cross_copy(z_at(4), half)
    t_both(t_last, 0)
    t_both(t_last, 1)
    t_both(t_last, 3)
    t_both(t_last, 2)
    text_swap = copy(tbig, tother, xsem.at[0], xsem.at[1], twin)

    def other_image(k, carry):
        wait_on(half_of(ibig, oc * 8 + k, 0), icross.at[k])
        wait_on(half_of(ibig, oc * 8 + k, 1), icross.at[8 + k])
        return carry

    lax.fori_loop(0, 8, other_image, 0)

    scale = scale_ref[0]

    def score(tile, carry):
        cols = pl.ds(pl.multiple_of(tile * WIDE, WIDE), WIDE)
        part = lax.dot_general(
            ibig[...], tbig[cols, :], (((1,), (1,)), ((), ())), preferred_element_type=jnp.float32
        )
        pad = lax.bitwise_and(lax.broadcasted_iota(jnp.int32, (1, WIDE), 1), PITCH - 1) >= ROWS
        logits[:, cols] = jnp.where(pad, FLOOR, part * scale)
        return carry

    lax.fori_loop(0, 4, score, 0)
    text_swap.start()

    def rows_of(k):
        return pl.ds(pl.multiple_of(k * PITCH, PITCH), ROWS)

    cmax[...] = jnp.full_like(cmax, FLOOR)

    def col_max(k, carry):
        cmax[...] = jnp.maximum(cmax[...], jnp.max(logits[rows_of(k), :].reshape(7, 8, TILE), 0))
        return carry

    lax.fori_loop(0, SIDE, col_max, 0)
    col_top = jnp.max(cmax[...], 0, keepdims=True)
    csum[...] = jnp.zeros_like(csum)

    first = lax.broadcasted_iota(jnp.int32, (ROWS, 128), 1) == 0

    def exponentials(g, carry):
        blocks = [rows_of(4 * g + q) for q in range(4)]
        tops = [jnp.max(logits[rows, :], 1, keepdims=True) for rows in blocks]
        added = jnp.zeros((8, TILE), jnp.float32)
        totals = []
        for rows, top in zip(blocks, tops):
            part = logits[rows, :]
            by_row = jnp.exp(part - top)
            by_col = jnp.exp(part - col_top)
            prow[rows, :] = by_row
            pcol[rows, :] = by_col
            added = added + jnp.sum(by_col.reshape(7, 8, TILE), 0)
            totals.append(jnp.sum(by_row, 1, keepdims=True))
        for rows, top, total in zip(blocks, tops, totals):
            rsub[rows, :] = jnp.where(first, top, total)
        csum[...] += added
        return carry

    lax.fori_loop(0, SIDE // 4, exponentials, 0)

    row_stats = jnp.transpose(rsub[...], (1, 0))
    col_total_here = jnp.sum(csum[...], 0, keepdims=True)
    for k in range(4):
        part = slice(k * WIDE, (k + 1) * WIDE)
        rmsg[k:k + 1, :] = row_stats[0:1, part]
        rmsg[4 + k:5 + k, :] = row_stats[1:2, part]
        cmsg[k:k + 1, :] = col_top[:, part]
        cmsg[4 + k:5 + k, :] = col_total_here[:, part]

    def spread(msg, stats, which, mine, peer_of):
        stats[mine] = msg[...]

        def send(k, carry):
            copy(msg, stats.at[mine], small_send.at[which], small_recv.at[which], peer_of(lax.rem(mine + k, SIDE))).start()
            return carry

        lax.fori_loop(1, SIDE, send, 0)

    def collect(stats, which):
        wait_on(stats.at[pl.ds(0, SIDE - 1)], small_recv.at[which])

    spread(rmsg, rstats, 0, islot, row_peer)
    spread(cmsg, cstats, 1, tslot, col_peer)

    def diagonal_slot(k):
        row_block = (x_lo * 2 + lax.div(k, 8)) * 64 + (y * 8 + lax.rem(k, 8)) * 2 + x_hi
        here = jnp.logical_and(lax.rem(row_block, 2) == c, lax.rem(lax.div(row_block, 8), 8) == z)
        slot = (lax.rem(lax.div(row_block, 4), 2) * 2 + lax.rem(lax.div(row_block, 2), 2)) * 4 + lax.div(row_block, 64)
        return here, slot

    def pair_mask(slot):
        row = lax.broadcasted_iota(jnp.int32, (ROWS, 128), 0)
        lane = lax.broadcasted_iota(jnp.int32, (ROWS, 128), 1)
        return lane == row + lax.rem(slot, 2) * PITCH

    def pair_cols(slot):
        return pl.ds(pl.multiple_of(lax.div(slot, 2) * 128, 128), 128)

    dsum[...] = jnp.zeros_like(dsum)

    def diagonal_logits(k, carry):
        here, slot = diagonal_slot(k)

        @pl.when(here)
        def _():
            picked = jnp.where(pair_mask(slot), logits[rows_of(k), pair_cols(slot)], 0.0)
            dsum[...] += jnp.sum(picked.reshape(7, 8, 128), 0)

        return carry

    lax.fori_loop(0, SIDE, diagonal_logits, 0)
    collect(rstats, 0)

    def combine(stats, mine):
        peaks = stats[:, 0:4, :]
        totals = stats[:, 4:8, :]
        peak = jnp.max(peaks, 0)
        total = jnp.sum(totals * jnp.exp(peaks - peak[None]), 0)
        factor = 0.5 * jnp.exp(mine[0:4, :] - peak) / total
        return peak + jnp.log(total), factor

    def line(v):
        return jnp.concatenate([v[k:k + 1, :] for k in range(4)], 1)

    row_lse, row_factor = combine(rstats, rmsg)
    frow[...] = jnp.transpose(jnp.broadcast_to(line(row_factor), (128, TILE)), (1, 0))
    collect(cstats, 1)
    col_lse, col_factor = combine(cstats, cmsg)
    csum[0:1, :] = line(col_factor)

    def weigh(k, carry):
        factor = frow[rows_of(k), :][:, 0:1]
        w = factor * prow[rows_of(k), :] + csum[0:1, :] * pcol[rows_of(k), :]
        weights[rows_of(k), :] = w.astype(jnp.bfloat16)
        here, slot = diagonal_slot(k)

        @pl.when(here)
        def _():
            cols = pair_cols(slot)
            v = frow[rows_of(k), :] * prow[rows_of(k), cols] + csum[0:1, cols] * pcol[rows_of(k), cols]
            v = v - jnp.where(pair_mask(slot), 1.0, 0.0)
            weights[rows_of(k), cols] = v.astype(jnp.bfloat16)

        return carry

    lax.fori_loop(oc * 8, oc * 8 + 8, weigh, 0)
    weight_swap = copy(
        weights.at[pl.ds(pl.multiple_of(oc * CORE, CORE), CORE), :], wother, xsem.at[2], xsem.at[3], twin
    )
    weight_swap.start()
    lax.fori_loop(c * 8, c * 8 + 8, weigh, 0)

    index = lax.broadcasted_iota(jnp.int32, (4, WIDE), 0) * WIDE + lax.broadcasted_iota(jnp.int32, (4, WIDE), 1)
    slot_of = lax.shift_right_logical(index, 6)
    valid = lax.bitwise_and(index, PITCH - 1) < ROWS
    terms = jnp.where(valid & (slot_of == islot), row_lse, 0.0) + jnp.where(valid & (slot_of == tslot), col_lse, 0.0)
    term = jnp.sum(jnp.sum(terms, 0, keepdims=True), 1, keepdims=True)
    diagonal = jnp.sum(jnp.sum(dsum[...], 0, keepdims=True), 1, keepdims=True)
    lmsg[...] = jnp.broadcast_to(term - 2.0 * diagonal, (8, 128))
    spread(lmsg, lstats, 2, islot, row_peer)

    for k in range(TILE // 128):
        wturned[:, k * 128:(k + 1) * 128] = jnp.transpose(weights[k * 128:(k + 1) * 128, :], (1, 0))

    def first_peer(axis, f):
        return device(x, f, z, c) if axis == 0 else device(f, y, z, c)

    def second_peer(axis, s):
        return device(s, y, z, c) if axis == 0 else device(x, s, z, c)

    def slab_copy(p, d):
        axis, _, width, at = PIECES[p]
        me = y if axis == 0 else x
        there = lax.rem(me + d, 4)
        cols = pl.ds(at, width)
        return copy(
            sout.at[axis, there, :, :, cols], sin.at[axis, d - 1, :, :, cols],
            ssend.at[0], srecv.at[p], first_peer(axis, there),
        )

    def text_terms(n):
        low = n * WIDE
        tpart[:, low:low + WIDE] = jnp.dot(wturned[...], ibig[:, low:low + WIDE], preferred_element_type=jnp.float32)
        for p, (axis, col, width, at) in enumerate(PIECES):
            if col // WIDE != n:
                continue
            for m in range(SIDE):
                first, second = (m % 4, m // 4) if axis == 0 else (m // 4, m % 4)
                piece = tpart[m * PITCH:m * PITCH + ROWS, col:col + width]
                sout[axis, first, second, :, at:at + width] = piece.astype(jnp.bfloat16)
            for d in (2, 1, 3):
                slab_copy(p, d).start()

    def keep_copy(p, d):
        axis, _, width, at = PIECES[p]
        me = x if axis == 0 else y
        there = lax.rem(me + d, 4)
        cols = pl.ds(at, width)
        return copy(
            pout.at[axis, there, :, cols], pin.at[axis, d - 1, :, cols],
            psend.at[0], precv.at[p], second_peer(axis, there),
        )

    def text_second(p):
        axis, col, width, at = PIECES[p]
        wait_on(sin.at[axis, pl.ds(0, 3), :, :, pl.ds(at, width)], srecv.at[p])
        me = x if axis == 0 else y
        for d in (2, 1, 3, 0):
            s = lax.rem(me + d, 4)
            m = s * 4 + y if axis == 0 else x * 4 + s
            total = tpart[rows_of(m), col:col + width]
            for e in range(3):
                total = total + sin[axis, e, s, :, at:at + width].astype(jnp.float32)
            if d == 0:
                pkeep[:, col:col + width] = total
            else:
                pout[axis, s, :, at:at + width] = total.astype(jnp.bfloat16)
                keep_copy(p, d).start()

    def text_last(p):
        axis, col, width, at = PIECES[p]
        wait_on(pin.at[axis, pl.ds(0, 3), :, pl.ds(at, width)], precv.at[p])
        total = pkeep[:, col:col + width]
        for d in range(3):
            total = total + pin[axis, d, :, at:at + width].astype(jnp.float32)
        tgrad_ref[:, col:col + width] = total

    def image_send(n, src, slot, low, width, sem, d):
        return copy(
            src, zin.at[slot, :, pl.ds(low, width)], zosend.at[0], sem.at[n], device(x, y, z_at(d), c)
        )

    def image_terms(n):
        low = n * WIDE
        cols = pl.ds(low, WIDE)
        mine = pl.ds(pl.multiple_of(c * CORE, CORE), CORE)
        part = jnp.dot(weights[mine, :], tbig[:, cols], preferred_element_type=jnp.float32)
        ipart[:, cols] = part + jnp.dot(wother[...], tother[:, cols], preferred_element_type=jnp.float32)
        for d in (3, -3, 4, 1, -1):
            zout[z_at(d), :, cols] = ipart[rows_of(z_at(d)), cols].astype(jnp.bfloat16)
        image_send(n, zout.at[z_at(4), :, pl.ds(low, 128)], 2, low, 128, zfirst, 2).start()
        image_send(n, zout.at[z_at(4), :, pl.ds(low + 128, 128)], 2, low + 128, 128, zfirst, -2).start()
        image_send(n, zout.at[z_at(3), :, cols], 0, low, WIDE, zfirst, 1).start()
        image_send(n, zout.at[z_at(-3), :, cols], 1, low, WIDE, zfirst, -1).start()
        image_send(n, zout.at[z_at(1), :, cols], 3, low, WIDE, zlast, 1).start()
        image_send(n, zout.at[z_at(-1), :, cols], 4, low, WIDE, zlast, -1).start()

    def image_second(n):
        low = n * WIDE
        cols = pl.ds(low, WIDE)
        wait_on(zin.at[pl.ds(0, 3), :, cols], zfirst.at[n])
        for way in range(2):
            d = 2 if way == 0 else -2
            total = ipart[rows_of(z_at(d)), cols] + zin[way, :, cols].astype(jnp.float32)
            edge = low + way * 128
            side = total[:, way * 128:way * 128 + 128] + zin[2, :, edge:edge + 128].astype(jnp.float32)
            rest = low + 128 - way * 128
            zagg[way, :, edge:edge + 128] = side.astype(jnp.bfloat16)
            zagg[way, :, rest:rest + 128] = total[:, 128 - way * 128:256 - way * 128].astype(jnp.bfloat16)
            image_send(n, zagg.at[way, :, cols], 5 + way, low, WIDE, zlast, d).start()

    def image_last(n):
        cols = pl.ds(n * WIDE, WIDE)
        wait_on(zin.at[pl.ds(3, 4), :, cols], zlast.at[n])
        total = ipart[rows_of(z), cols]
        for k in range(3, 7):
            total = total + zin[k, :, cols].astype(jnp.float32)
        igrad_ref[:, cols] = total

    text_terms(0)
    text_swap.wait()
    weight_swap.wait()
    image_terms(0)
    text_terms(1)
    image_terms(1)
    image_second(0)
    text_terms(2)
    image_terms(2)
    image_second(1)
    text_second(0)
    text_terms(3)
    image_terms(3)
    image_second(2)
    text_second(1)
    text_terms(4)
    image_terms(4)
    image_second(3)
    text_second(2)
    collect(lstats, 2)
    pmsg[...] = jnp.sum(lstats[...], 0)
    spread(pmsg, pstats, 3, tslot, col_peer)
    image_second(4)
    text_second(3)
    text_second(4)
    text_second(5)
    for n in range(CHUNKS):
        image_last(n)
        text_last(n)
    text_last(5)
    collect(pstats, 3)
    loss_ref[...] = (jnp.sum(pstats[...], 0) / (2.0 * PAIRS))[0:1, 0:1]

    wait_on(ibig.at[pl.ds(0, 7 * PITCH), :], zsend.at[0])
    wait_on(ibig.at[pl.ds(0, 8 * PITCH), :], isend.at[0])
    wait_on(tbig.at[pl.ds(0, 15 * PITCH), :], tsend.at[0])
    wait_on(rstats.at[pl.ds(0, SIDE - 1)], small_send.at[0])
    wait_on(cstats.at[pl.ds(0, SIDE - 1)], small_send.at[1])
    wait_on(lstats.at[pl.ds(0, SIDE - 1)], small_send.at[2])
    wait_on(pstats.at[pl.ds(0, SIDE - 1)], small_send.at[3])
    wait_on(zin, zosend.at[0])
    wait_on(sout.at[:, pl.ds(0, 3)], ssend.at[0])
    wait_on(pout.at[:, pl.ds(0, 3)], psend.at[0])


def per_device(images, texts, logit_scale):
    f32, bf16 = jnp.float32, jnp.bfloat16
    dma = pltpu.SemaphoreType.DMA
    vmem = pl.BlockSpec(memory_space=pltpu.VMEM)
    smem = pl.BlockSpec(memory_space=pltpu.SMEM)
    hbm = pl.BlockSpec(memory_space=pl.ANY)
    loss, image_grad, text_grad = pl.pallas_call(
        kernel,
        out_shape=(
            jax.ShapeDtypeStruct((1, 1), f32),
            jax.ShapeDtypeStruct((ROWS, E), f32),
            jax.ShapeDtypeStruct((ROWS, E), f32),
        ),
        in_specs=[hbm, hbm, smem],
        out_specs=(vmem, vmem, vmem),
        scratch_shapes=[
            pltpu.VMEM((2, ROWS, E), bf16),
            pltpu.VMEM((TILE, E), bf16),
            pltpu.VMEM((TILE, E), bf16),
            pltpu.VMEM((TILE, E), bf16),
            pltpu.VMEM((TILE, TILE), f32),
            pltpu.VMEM((TILE, TILE), f32),
            pltpu.VMEM((TILE, TILE), f32),
            pltpu.VMEM((TILE, TILE), bf16),
            pltpu.VMEM((CORE, TILE), bf16),
            pltpu.VMEM((TILE, TILE), bf16),
            pltpu.VMEM((TILE, 128), f32),
            pltpu.VMEM((8, TILE), f32),
            pltpu.VMEM((8, TILE), f32),
            pltpu.VMEM((8, 128), f32),
            pltpu.VMEM((TILE, 128), f32),
            pltpu.VMEM((8, WIDE), f32),
            pltpu.VMEM((8, WIDE), f32),
            pltpu.VMEM((SIDE, 8, WIDE), f32),
            pltpu.VMEM((SIDE, 8, WIDE), f32),
            pltpu.VMEM((8, 128), f32),
            pltpu.VMEM((SIDE, 8, 128), f32),
            pltpu.VMEM((8, 128), f32),
            pltpu.VMEM((SIDE, 8, 128), f32),
            pltpu.VMEM((CORE, E), f32),
            pltpu.VMEM((TILE, E), f32),
            pltpu.VMEM((8, ROWS, E), bf16),
            pltpu.VMEM((2, ROWS, E), bf16),
            pltpu.VMEM((7, ROWS, E), bf16),
            pltpu.VMEM((2, 4, 4, ROWS, HALF), bf16),
            pltpu.VMEM((2, 3, 4, ROWS, HALF), bf16),
            pltpu.VMEM((2, 4, ROWS, HALF), bf16),
            pltpu.VMEM((2, 3, ROWS, HALF), bf16),
            pltpu.VMEM((ROWS, E), f32),
            dma((2,)), dma((1,)), dma((16,)), dma((1,)), dma((16,)),
            dma((1,)), dma((8,)), dma((8,)), dma((8,)), dma((8,)), dma((4,)),
            dma((4,)), dma((4,)), dma((1,)), dma((5,)), dma((5,)),
            dma((1,)), dma((6,)), dma((1,)), dma((6,)),
        ],
        compiler_params=pltpu.CompilerParams(
            collective_id=0, has_side_effects=True, vmem_limit_bytes=60 * 1024 * 1024
        ),
    )(images, texts, logit_scale)
    return loss.reshape(1), image_grad, text_grad


def solution(mesh):
    in_specs = (P(("img", "txt"), None), P(("txt", "img"), None), P())
    out_specs = (P(), P(("img", "txt"), None), P(("txt", "img"), None))
    return jax.shard_map(
        per_device, mesh=mesh, in_specs=in_specs, out_specs=out_specs, check_vma=False
    )
```

```python
import jax
import jax.numpy as jnp
from jax import lax
from jax.experimental import pallas as pl
from jax.experimental.pallas import tpu as pltpu
from jax.sharding import PartitionSpec as P

MESH = pl.DeviceIdType.MESH
ROWS = 56
PITCH = 64
SIDE = 16
TILE = SIDE * PITCH
CORE = 8 * PITCH
E = 1280
PAIRS = 14336
WIDE = 256
CHUNKS = E // WIDE
HALF = 640
FLOOR = -1e30
PIECES = (
    (0, 0, 256, 0),
    (1, 256, 256, 0),
    (0, 512, 256, 256),
    (1, 768, 256, 256),
    (0, 1024, 128, 512),
    (1, 1152, 128, 512),
)
NEAR = (1, 3, 2)


def device(x, y, z, c):
    return (lax.rem(x, 2) * 2 + c, (y * 8 + z) * 2 + lax.div(x, 2))


def kernel(
    images_ref, texts_ref, scale_ref,
    loss_ref, igrad_ref, tgrad_ref,
    stage, ibig, tbig, tother, logits, prow, pcol, weights, wother, wturned,
    rsub, csum, cmax, dsum, frow, rmsg, cmsg, rstats, cstats, lmsg, lstats, pmsg, pstats,
    ipart, tpart, zout, zagg, zin, sout, sin, pout, pin, pkeep,
    own_sem, zsend, zrecv, isend, icross, tsend, tfirst, tplus, tminus, tfar, xsem,
    small_send, small_recv, zosend, zfirst, zlast, ssend, srecv, psend, precv,
):
    img = lax.axis_index("img")
    txt = lax.axis_index("txt")
    x_lo = lax.div(img, 2)
    c = lax.rem(img, 2)
    x_hi = lax.rem(txt, 2)
    x = x_hi * 2 + x_lo
    y = lax.div(txt, 16)
    z = lax.rem(lax.div(txt, 2), 8)
    oc = 1 - c
    islot = c * 8 + z
    tslot = x * 4 + y

    def x_at(d):
        return lax.rem(x + d, 4)

    def y_at(d):
        return lax.rem(y + d, 4)

    def z_at(d):
        return lax.rem(z + d + 8, 8)

    def row_peer(slot):
        return device(x, y, lax.rem(slot, 8), lax.div(slot, 8))

    def col_peer(slot):
        return device(lax.div(slot, 4), lax.rem(slot, 4), z, c)

    twin = device(x, y, z, oc)

    def copy(src, dst, send, recv, where):
        return pltpu.make_async_remote_copy(
            src_ref=src, dst_ref=dst, send_sem=send, recv_sem=recv,
            device_id=where, device_id_type=MESH,
        )

    def wait_on(ref, sem):
        copy(ref, ref, sem, sem, twin).wait_recv()

    barrier = pltpu.get_barrier_semaphore()

    def greet(k, carry):
        pl.semaphore_signal(barrier, inc=1, device_id=row_peer(lax.rem(islot + k, SIDE)), device_id_type=MESH)
        pl.semaphore_signal(barrier, inc=1, device_id=col_peer(lax.rem(tslot + k, SIDE)), device_id_type=MESH)
        return carry

    lax.fori_loop(1, SIDE, greet, 0)
    own_image = pltpu.make_async_copy(images_ref, stage.at[0], own_sem.at[0])
    own_text = pltpu.make_async_copy(texts_ref, stage.at[1], own_sem.at[1])
    own_image.start()
    own_text.start()

    def block_rows(slot):
        return pl.ds(pl.multiple_of(slot * PITCH, PITCH), PITCH)

    ibig[block_rows(islot), :] = jnp.zeros((PITCH, E), jnp.bfloat16)
    tbig[block_rows(tslot), :] = jnp.zeros((PITCH, E), jnp.bfloat16)
    own_image.wait()
    own_text.wait()
    ibig[pl.ds(pl.multiple_of(islot * PITCH, PITCH), ROWS), :] = stage[0]
    tbig[pl.ds(pl.multiple_of(tslot * PITCH, PITCH), ROWS), :] = stage[1]
    pl.semaphore_wait(barrier, 2 * (SIDE - 1))

    def half_of(big, slot, half):
        return big.at[block_rows(slot), pl.ds(half * HALF, HALF)]

    def z_copy(owner, way, half, far=False):
        ref = half_of(ibig, c * 8 + owner, half)
        d = 2 if far else 1
        return copy(ref, ref, zsend.at[0], zrecv.at[half * 8 + owner], device(x, y, z_at(d if way == 0 else -d), c))

    def z_wait(owner, half):
        wait_on(half_of(ibig, c * 8 + owner, half), zrecv.at[half * 8 + owner])

    def cross_copy(owner, half):
        ref = half_of(ibig, c * 8 + owner, half)
        copy(ref, ref, isend.at[0], icross.at[half * 8 + owner], twin).start()

    def t_slot(half, u, v):
        return u * 4 + v if half == 0 else v * 4 + u

    def t_here(half):
        return (x, y) if half == 0 else (y, x)

    def t_device(half, u, v):
        return device(u, v, z, c) if half == 0 else device(v, u, z, c)

    def t_send(half, u, v, sem, to_u, to_v):
        ref = half_of(tbig, t_slot(half, u, v), half)
        copy(ref, ref, tsend.at[0], sem.at[half * 4 + u], t_device(half, to_u, to_v)).start()

    def t_wait(half, u, v, sem):
        wait_on(half_of(tbig, t_slot(half, u, v), half), sem.at[half * 4 + u])

    def t_first(half):
        u, v = t_here(half)
        for d in NEAR:
            t_send(half, u, v, tfirst, lax.rem(u + d, 4), v)

    def t_second(half, d):
        u, v = t_here(half)
        there = lax.rem(u + d, 4)
        if d:
            t_wait(half, there, v, tfirst)
        if d == 2:
            t_send(half, there, v, tfar, u, lax.rem(v + 2, 4))
        t_send(half, there, v, tplus, u, lax.rem(v + 1, 4))
        t_send(half, there, v, tminus, u, lax.rem(v + 3, 4))

    def t_pass(half, d):
        u, v = t_here(half)
        there = lax.rem(u + d, 4)
        before = lax.rem(v + 3, 4)
        after = lax.rem(v + 1, 4)
        t_wait(half, there, before, tplus)
        if d < 2:
            t_send(half, there, before, tfar, u, after)
        t_wait(half, there, after, tminus)
        if d == 3:
            t_send(half, there, after, tfar, u, before)

    def t_last(half, d):
        u, v = t_here(half)
        t_wait(half, lax.rem(u + d, 4), lax.rem(v + 2, 4), tfar)

    t_first(0)
    t_first(1)
    z_copy(z, 0, 0).start()
    z_copy(z, 1, 0).start()
    t_second(0, 0)
    t_second(1, 0)
    z_copy(z, 0, 1).start()
    z_copy(z, 1, 1).start()
    cross_copy(z, 0)
    cross_copy(z, 1)
    weights[...] = jnp.zeros_like(weights)
    rsub[...] = jnp.zeros_like(rsub)

    def z_step(step, half):
        left = z_at(-1 - step)
        right = z_at(1 + step)
        z_wait(left, half)
        if step == 1:
            @pl.when(c == 0)
            def _():
                z_copy(left, 0, half, True).start()
        if step < 2:
            z_copy(left, 0, half).start()
        cross_copy(left, half)
        z_wait(right, half)
        if step == 1:
            @pl.when(c == 1)
            def _():
                z_copy(right, 1, half, True).start()
        if step < 2:
            z_copy(right, 1, half).start()
        cross_copy(right, half)

    def t_both(what, d):
        what(0, d)
        what(1, d)

    z_step(0, 0)
    t_both(t_second, 1)
    t_both(t_second, 3)
    z_step(0, 1)
    t_both(t_second, 2)
    z_step(1, 0)
    t_both(t_pass, 0)
    z_step(1, 1)
    t_both(t_pass, 1)
    t_both(t_pass, 3)
    z_step(2, 0)
    z_step(2, 1)
    t_both(t_pass, 2)
    for half in range(2):
        z_wait(z_at(4), half)
        cross_copy(z_at(4), half)
    t_both(t_last, 0)
    t_both(t_last, 1)
    t_both(t_last, 3)
    t_both(t_last, 2)
    text_swap = copy(tbig, tother, xsem.at[0], xsem.at[1], twin)

    def other_image(k, carry):
        wait_on(half_of(ibig, oc * 8 + k, 0), icross.at[k])
        wait_on(half_of(ibig, oc * 8 + k, 1), icross.at[8 + k])
        return carry

    lax.fori_loop(0, 8, other_image, 0)

    scale = scale_ref[0]

    def score(tile, carry):
        cols = pl.ds(pl.multiple_of(tile * WIDE, WIDE), WIDE)
        part = lax.dot_general(
            ibig[...], tbig[cols, :], (((1,), (1,)), ((), ())), preferred_element_type=jnp.float32
        )
        pad = lax.bitwise_and(lax.broadcasted_iota(jnp.int32, (1, WIDE), 1), PITCH - 1) >= ROWS
        logits[:, cols] = jnp.where(pad, FLOOR, part * scale)
        return carry

    lax.fori_loop(0, 4, score, 0)
    text_swap.start()

    def rows_of(k):
        return pl.ds(pl.multiple_of(k * PITCH, PITCH), ROWS)

    cmax[...] = jnp.full_like(cmax, FLOOR)

    def col_max(k, carry):
        cmax[...] = jnp.maximum(cmax[...], jnp.max(logits[rows_of(k), :].reshape(7, 8, TILE), 0))
        return carry

    lax.fori_loop(0, SIDE, col_max, 0)
    col_top = jnp.max(cmax[...], 0, keepdims=True)
    csum[...] = jnp.zeros_like(csum)

    first = lax.broadcasted_iota(jnp.int32, (ROWS, 128), 1) == 0

    def exponentials(g, carry):
        blocks = [rows_of(4 * g + q) for q in range(4)]
        tops = [jnp.max(logits[rows, :], 1, keepdims=True) for rows in blocks]
        added = jnp.zeros((8, TILE), jnp.float32)
        totals = []
        for rows, top in zip(blocks, tops):
            part = logits[rows, :]
            by_row = jnp.exp(part - top)
            by_col = jnp.exp(part - col_top)
            prow[rows, :] = by_row
            pcol[rows, :] = by_col
            added = added + jnp.sum(by_col.reshape(7, 8, TILE), 0)
            totals.append(jnp.sum(by_row, 1, keepdims=True))
        for rows, top, total in zip(blocks, tops, totals):
            rsub[rows, :] = jnp.where(first, top, total)
        csum[...] += added
        return carry

    lax.fori_loop(0, SIDE // 4, exponentials, 0)

    row_stats = jnp.transpose(rsub[...], (1, 0))
    col_total_here = jnp.sum(csum[...], 0, keepdims=True)
    for k in range(4):
        part = slice(k * WIDE, (k + 1) * WIDE)
        rmsg[k:k + 1, :] = row_stats[0:1, part]
        rmsg[4 + k:5 + k, :] = row_stats[1:2, part]
        cmsg[k:k + 1, :] = col_top[:, part]
        cmsg[4 + k:5 + k, :] = col_total_here[:, part]

    def spread(msg, stats, which, mine, peer_of):
        stats[mine] = msg[...]

        def send(k, carry):
            copy(msg, stats.at[mine], small_send.at[which], small_recv.at[which], peer_of(lax.rem(mine + k, SIDE))).start()
            return carry

        lax.fori_loop(1, SIDE, send, 0)

    def collect(stats, which):
        wait_on(stats.at[pl.ds(0, SIDE - 1)], small_recv.at[which])

    spread(rmsg, rstats, 0, islot, row_peer)
    spread(cmsg, cstats, 1, tslot, col_peer)

    def diagonal_slot(k):
        row_block = (x_lo * 2 + lax.div(k, 8)) * 64 + (y * 8 + lax.rem(k, 8)) * 2 + x_hi
        here = jnp.logical_and(lax.rem(row_block, 2) == c, lax.rem(lax.div(row_block, 8), 8) == z)
        slot = (lax.rem(lax.div(row_block, 4), 2) * 2 + lax.rem(lax.div(row_block, 2), 2)) * 4 + lax.div(row_block, 64)
        return here, slot

    def pair_mask(slot):
        row = lax.broadcasted_iota(jnp.int32, (ROWS, 128), 0)
        lane = lax.broadcasted_iota(jnp.int32, (ROWS, 128), 1)
        return lane == row + lax.rem(slot, 2) * PITCH

    def pair_cols(slot):
        return pl.ds(pl.multiple_of(lax.div(slot, 2) * 128, 128), 128)

    dsum[...] = jnp.zeros_like(dsum)

    def diagonal_logits(k, carry):
        here, slot = diagonal_slot(k)

        @pl.when(here)
        def _():
            picked = jnp.where(pair_mask(slot), logits[rows_of(k), pair_cols(slot)], 0.0)
            dsum[...] += jnp.sum(picked.reshape(7, 8, 128), 0)

        return carry

    lax.fori_loop(0, SIDE, diagonal_logits, 0)
    collect(rstats, 0)

    def combine(stats, mine):
        peaks = stats[:, 0:4, :]
        totals = stats[:, 4:8, :]
        peak = jnp.max(peaks, 0)
        total = jnp.sum(totals * jnp.exp(peaks - peak[None]), 0)
        factor = 0.5 * jnp.exp(mine[0:4, :] - peak) / total
        return peak + jnp.log(total), factor

    def line(v):
        return jnp.concatenate([v[k:k + 1, :] for k in range(4)], 1)

    row_lse, row_factor = combine(rstats, rmsg)
    frow[...] = jnp.transpose(jnp.broadcast_to(line(row_factor), (128, TILE)), (1, 0))
    collect(cstats, 1)
    col_lse, col_factor = combine(cstats, cmsg)
    csum[0:1, :] = line(col_factor)

    def weigh(k, carry):
        factor = frow[rows_of(k), :][:, 0:1]
        w = factor * prow[rows_of(k), :] + csum[0:1, :] * pcol[rows_of(k), :]
        weights[rows_of(k), :] = w.astype(jnp.bfloat16)
        here, slot = diagonal_slot(k)

        @pl.when(here)
        def _():
            cols = pair_cols(slot)
            v = frow[rows_of(k), :] * prow[rows_of(k), cols] + csum[0:1, cols] * pcol[rows_of(k), cols]
            v = v - jnp.where(pair_mask(slot), 1.0, 0.0)
            weights[rows_of(k), cols] = v.astype(jnp.bfloat16)

        return carry

    lax.fori_loop(oc * 8, oc * 8 + 8, weigh, 0)
    weight_swap = copy(
        weights.at[pl.ds(pl.multiple_of(oc * CORE, CORE), CORE), :], wother, xsem.at[2], xsem.at[3], twin
    )
    weight_swap.start()
    lax.fori_loop(c * 8, c * 8 + 8, weigh, 0)

    index = lax.broadcasted_iota(jnp.int32, (4, WIDE), 0) * WIDE + lax.broadcasted_iota(jnp.int32, (4, WIDE), 1)
    slot_of = lax.shift_right_logical(index, 6)
    valid = lax.bitwise_and(index, PITCH - 1) < ROWS
    terms = jnp.where(valid & (slot_of == islot), row_lse, 0.0) + jnp.where(valid & (slot_of == tslot), col_lse, 0.0)
    term = jnp.sum(jnp.sum(terms, 0, keepdims=True), 1, keepdims=True)
    diagonal = jnp.sum(jnp.sum(dsum[...], 0, keepdims=True), 1, keepdims=True)
    lmsg[...] = jnp.broadcast_to(term - 2.0 * diagonal, (8, 128))
    spread(lmsg, lstats, 2, islot, row_peer)

    for k in range(TILE // 128):
        wturned[:, k * 128:(k + 1) * 128] = jnp.transpose(weights[k * 128:(k + 1) * 128, :], (1, 0))

    def first_peer(axis, f):
        return device(x, f, z, c) if axis == 0 else device(f, y, z, c)

    def second_peer(axis, s):
        return device(s, y, z, c) if axis == 0 else device(x, s, z, c)

    def slab_copy(p, d):
        axis, _, width, at = PIECES[p]
        me = y if axis == 0 else x
        there = lax.rem(me + d, 4)
        cols = pl.ds(at, width)
        return copy(
            sout.at[axis, there, :, :, cols], sin.at[axis, d - 1, :, :, cols],
            ssend.at[0], srecv.at[p], first_peer(axis, there),
        )

    def text_terms(n):
        low = n * WIDE
        tpart[:, low:low + WIDE] = jnp.dot(wturned[...], ibig[:, low:low + WIDE], preferred_element_type=jnp.float32)
        for p, (axis, col, width, at) in enumerate(PIECES):
            if col // WIDE != n:
                continue
            for m in range(SIDE):
                first, second = (m % 4, m // 4) if axis == 0 else (m // 4, m % 4)
                piece = tpart[m * PITCH:m * PITCH + ROWS, col:col + width]
                sout[axis, first, second, :, at:at + width] = piece.astype(jnp.bfloat16)
            for d in (2, 1, 3):
                slab_copy(p, d).start()

    def keep_copy(p, d):
        axis, _, width, at = PIECES[p]
        me = x if axis == 0 else y
        there = lax.rem(me + d, 4)
        cols = pl.ds(at, width)
        return copy(
            pout.at[axis, there, :, cols], pin.at[axis, d - 1, :, cols],
            psend.at[0], precv.at[p], second_peer(axis, there),
        )

    def text_second(p):
        axis, col, width, at = PIECES[p]
        wait_on(sin.at[axis, pl.ds(0, 3), :, :, pl.ds(at, width)], srecv.at[p])
        me = x if axis == 0 else y
        for d in (2, 1, 3, 0):
            s = lax.rem(me + d, 4)
            m = s * 4 + y if axis == 0 else x * 4 + s
            total = tpart[rows_of(m), col:col + width]
            for e in range(3):
                total = total + sin[axis, e, s, :, at:at + width].astype(jnp.float32)
            if d == 0:
                pkeep[:, col:col + width] = total
            else:
                pout[axis, s, :, at:at + width] = total.astype(jnp.bfloat16)
                keep_copy(p, d).start()

    def text_last(p):
        axis, col, width, at = PIECES[p]
        wait_on(pin.at[axis, pl.ds(0, 3), :, pl.ds(at, width)], precv.at[p])
        total = pkeep[:, col:col + width]
        for d in range(3):
            total = total + pin[axis, d, :, at:at + width].astype(jnp.float32)
        tgrad_ref[:, col:col + width] = total

    def image_send(n, src, slot, low, width, sem, d):
        return copy(
            src, zin.at[slot, :, pl.ds(low, width)], zosend.at[0], sem.at[n], device(x, y, z_at(d), c)
        )

    def image_terms(n):
        low = n * WIDE
        cols = pl.ds(low, WIDE)
        mine = pl.ds(pl.multiple_of(c * CORE, CORE), CORE)
        part = jnp.dot(weights[mine, :], tbig[:, cols], preferred_element_type=jnp.float32)
        ipart[:, cols] = part + jnp.dot(wother[...], tother[:, cols], preferred_element_type=jnp.float32)
        for d in (3, -3, 4, 1, -1):
            zout[z_at(d), :, cols] = ipart[rows_of(z_at(d)), cols].astype(jnp.bfloat16)
        image_send(n, zout.at[z_at(4), :, pl.ds(low, 128)], 2, low, 128, zfirst, 2).start()
        image_send(n, zout.at[z_at(4), :, pl.ds(low + 128, 128)], 2, low + 128, 128, zfirst, -2).start()
        image_send(n, zout.at[z_at(3), :, cols], 0, low, WIDE, zfirst, 1).start()
        image_send(n, zout.at[z_at(-3), :, cols], 1, low, WIDE, zfirst, -1).start()

    def image_near(n):
        low = n * WIDE
        cols = pl.ds(low, WIDE)
        image_send(n, zout.at[z_at(1), :, cols], 3, low, WIDE, zlast, 1).start()
        image_send(n, zout.at[z_at(-1), :, cols], 4, low, WIDE, zlast, -1).start()

    def image_second(n):
        low = n * WIDE
        cols = pl.ds(low, WIDE)
        wait_on(zin.at[pl.ds(0, 3), :, cols], zfirst.at[n])
        for way in range(2):
            d = 2 if way == 0 else -2
            total = ipart[rows_of(z_at(d)), cols] + zin[way, :, cols].astype(jnp.float32)
            edge = low + way * 128
            side = total[:, way * 128:way * 128 + 128] + zin[2, :, edge:edge + 128].astype(jnp.float32)
            rest = low + 128 - way * 128
            zagg[way, :, edge:edge + 128] = side.astype(jnp.bfloat16)
            zagg[way, :, rest:rest + 128] = total[:, 128 - way * 128:256 - way * 128].astype(jnp.bfloat16)
            image_send(n, zagg.at[way, :, cols], 5 + way, low, WIDE, zlast, d).start()

    def image_last(n):
        cols = pl.ds(n * WIDE, WIDE)
        wait_on(zin.at[pl.ds(3, 4), :, cols], zlast.at[n])
        total = ipart[rows_of(z), cols]
        for k in range(3, 7):
            total = total + zin[k, :, cols].astype(jnp.float32)
        igrad_ref[:, cols] = total

    text_terms(0)
    text_terms(1)
    text_swap.wait()
    weight_swap.wait()
    image_terms(0)
    image_terms(1)
    text_terms(2)
    text_terms(3)
    image_terms(2)
    image_terms(3)
    text_terms(4)
    image_terms(4)
    image_second(0)
    image_near(0)
    text_second(0)
    image_second(1)
    image_near(1)
    text_second(1)
    image_second(2)
    image_near(2)
    text_second(2)
    image_second(3)
    image_near(3)
    text_second(3)
    collect(lstats, 2)
    pmsg[...] = jnp.sum(lstats[...], 0)
    spread(pmsg, pstats, 3, tslot, col_peer)
    image_second(4)
    image_near(4)
    text_second(4)
    text_second(5)
    for n in range(CHUNKS):
        image_last(n)
        text_last(n)
    text_last(5)
    collect(pstats, 3)
    loss_ref[...] = (jnp.sum(pstats[...], 0) / (2.0 * PAIRS))[0:1, 0:1]

    wait_on(ibig.at[pl.ds(0, 7 * PITCH), :], zsend.at[0])
    wait_on(ibig.at[pl.ds(0, 8 * PITCH), :], isend.at[0])
    wait_on(tbig.at[pl.ds(0, 15 * PITCH), :], tsend.at[0])
    wait_on(rstats.at[pl.ds(0, SIDE - 1)], small_send.at[0])
    wait_on(cstats.at[pl.ds(0, SIDE - 1)], small_send.at[1])
    wait_on(lstats.at[pl.ds(0, SIDE - 1)], small_send.at[2])
    wait_on(pstats.at[pl.ds(0, SIDE - 1)], small_send.at[3])
    wait_on(zin, zosend.at[0])
    wait_on(sout.at[:, pl.ds(0, 3)], ssend.at[0])
    wait_on(pout.at[:, pl.ds(0, 3)], psend.at[0])


def per_device(images, texts, logit_scale):
    f32, bf16 = jnp.float32, jnp.bfloat16
    dma = pltpu.SemaphoreType.DMA
    vmem = pl.BlockSpec(memory_space=pltpu.VMEM)
    smem = pl.BlockSpec(memory_space=pltpu.SMEM)
    hbm = pl.BlockSpec(memory_space=pl.ANY)
    loss, image_grad, text_grad = pl.pallas_call(
        kernel,
        out_shape=(
            jax.ShapeDtypeStruct((1, 1), f32),
            jax.ShapeDtypeStruct((ROWS, E), f32),
            jax.ShapeDtypeStruct((ROWS, E), f32),
        ),
        in_specs=[hbm, hbm, smem],
        out_specs=(vmem, vmem, vmem),
        scratch_shapes=[
            pltpu.VMEM((2, ROWS, E), bf16),
            pltpu.VMEM((TILE, E), bf16),
            pltpu.VMEM((TILE, E), bf16),
            pltpu.VMEM((TILE, E), bf16),
            pltpu.VMEM((TILE, TILE), f32),
            pltpu.VMEM((TILE, TILE), f32),
            pltpu.VMEM((TILE, TILE), f32),
            pltpu.VMEM((TILE, TILE), bf16),
            pltpu.VMEM((CORE, TILE), bf16),
            pltpu.VMEM((TILE, TILE), bf16),
            pltpu.VMEM((TILE, 128), f32),
            pltpu.VMEM((8, TILE), f32),
            pltpu.VMEM((8, TILE), f32),
            pltpu.VMEM((8, 128), f32),
            pltpu.VMEM((TILE, 128), f32),
            pltpu.VMEM((8, WIDE), f32),
            pltpu.VMEM((8, WIDE), f32),
            pltpu.VMEM((SIDE, 8, WIDE), f32),
            pltpu.VMEM((SIDE, 8, WIDE), f32),
            pltpu.VMEM((8, 128), f32),
            pltpu.VMEM((SIDE, 8, 128), f32),
            pltpu.VMEM((8, 128), f32),
            pltpu.VMEM((SIDE, 8, 128), f32),
            pltpu.VMEM((CORE, E), f32),
            pltpu.VMEM((TILE, E), f32),
            pltpu.VMEM((8, ROWS, E), bf16),
            pltpu.VMEM((2, ROWS, E), bf16),
            pltpu.VMEM((7, ROWS, E), bf16),
            pltpu.VMEM((2, 4, 4, ROWS, HALF), bf16),
            pltpu.VMEM((2, 3, 4, ROWS, HALF), bf16),
            pltpu.VMEM((2, 4, ROWS, HALF), bf16),
            pltpu.VMEM((2, 3, ROWS, HALF), bf16),
            pltpu.VMEM((ROWS, E), f32),
            dma((2,)), dma((1,)), dma((16,)), dma((1,)), dma((16,)),
            dma((1,)), dma((8,)), dma((8,)), dma((8,)), dma((8,)), dma((4,)),
            dma((4,)), dma((4,)), dma((1,)), dma((5,)), dma((5,)),
            dma((1,)), dma((6,)), dma((1,)), dma((6,)),
        ],
        compiler_params=pltpu.CompilerParams(
            collective_id=0, has_side_effects=True, vmem_limit_bytes=60 * 1024 * 1024
        ),
    )(images, texts, logit_scale)
    return loss.reshape(1), image_grad, text_grad


def solution(mesh):
    in_specs = (P(("img", "txt"), None), P(("txt", "img"), None), P())
    out_specs = (P(), P(("img", "txt"), None), P(("txt", "img"), None))
    return jax.shard_map(
        per_device, mesh=mesh, in_specs=in_specs, out_specs=out_specs, check_vma=False
    )
```

```python
import jax
import jax.numpy as jnp
from jax import lax
from jax.experimental import pallas as pl
from jax.experimental.pallas import tpu as pltpu
from jax.sharding import PartitionSpec as P

MESH = pl.DeviceIdType.MESH
ROWS = 56
PITCH = 64
SIDE = 16
TILE = SIDE * PITCH
CORE = 8 * PITCH
E = 1280
PAIRS = 14336
WIDE = 256
CHUNKS = E // WIDE
HALF = 640
FLOOR = -1e30
PIECES = tuple(
    (axis, n * WIDE + axis * 128, 128, n * 128) for n in range(CHUNKS) for axis in range(2)
)
NEAR = (1, 3, 2)


def device(x, y, z, c):
    return (lax.rem(x, 2) * 2 + c, (y * 8 + z) * 2 + lax.div(x, 2))


def kernel(
    images_ref, texts_ref, scale_ref,
    loss_ref, igrad_ref, tgrad_ref,
    stage, ibig, tbig, tother, logits, prow, pcol, weights, wother, wturned,
    rsub, csum, cmax, dsum, frow, rmsg, cmsg, rstats, cstats, lmsg, lstats, pmsg, pstats,
    ipart, tpart, zout, zagg, zin, sout, sin, pout, pin, pkeep,
    own_sem, zsend, zrecv, isend, icross, tsend, tfirst, tplus, tminus, tfar, xsem,
    small_send, small_recv, zosend, zfirst, zlast, ssend, srecv, psend, precv,
):
    img = lax.axis_index("img")
    txt = lax.axis_index("txt")
    x_lo = lax.div(img, 2)
    c = lax.rem(img, 2)
    x_hi = lax.rem(txt, 2)
    x = x_hi * 2 + x_lo
    y = lax.div(txt, 16)
    z = lax.rem(lax.div(txt, 2), 8)
    oc = 1 - c
    islot = c * 8 + z
    tslot = x * 4 + y

    def x_at(d):
        return lax.rem(x + d, 4)

    def y_at(d):
        return lax.rem(y + d, 4)

    def z_at(d):
        return lax.rem(z + d + 8, 8)

    def row_peer(slot):
        return device(x, y, lax.rem(slot, 8), lax.div(slot, 8))

    def col_peer(slot):
        return device(lax.div(slot, 4), lax.rem(slot, 4), z, c)

    twin = device(x, y, z, oc)

    def copy(src, dst, send, recv, where):
        return pltpu.make_async_remote_copy(
            src_ref=src, dst_ref=dst, send_sem=send, recv_sem=recv,
            device_id=where, device_id_type=MESH,
        )

    def wait_on(ref, sem):
        copy(ref, ref, sem, sem, twin).wait_recv()

    barrier = pltpu.get_barrier_semaphore()

    def greet(k, carry):
        pl.semaphore_signal(barrier, inc=1, device_id=row_peer(lax.rem(islot + k, SIDE)), device_id_type=MESH)
        pl.semaphore_signal(barrier, inc=1, device_id=col_peer(lax.rem(tslot + k, SIDE)), device_id_type=MESH)
        return carry

    lax.fori_loop(1, SIDE, greet, 0)
    own_image = pltpu.make_async_copy(images_ref, stage.at[0], own_sem.at[0])
    own_text = pltpu.make_async_copy(texts_ref, stage.at[1], own_sem.at[1])
    own_image.start()
    own_text.start()

    def block_rows(slot):
        return pl.ds(pl.multiple_of(slot * PITCH, PITCH), PITCH)

    ibig[block_rows(islot), :] = jnp.zeros((PITCH, E), jnp.bfloat16)
    tbig[block_rows(tslot), :] = jnp.zeros((PITCH, E), jnp.bfloat16)
    own_image.wait()
    own_text.wait()
    ibig[pl.ds(pl.multiple_of(islot * PITCH, PITCH), ROWS), :] = stage[0]
    tbig[pl.ds(pl.multiple_of(tslot * PITCH, PITCH), ROWS), :] = stage[1]
    pl.semaphore_wait(barrier, 2 * (SIDE - 1))

    def half_of(big, slot, half):
        return big.at[block_rows(slot), pl.ds(half * HALF, HALF)]

    def z_copy(owner, way, half, far=False):
        ref = half_of(ibig, c * 8 + owner, half)
        d = 2 if far else 1
        return copy(ref, ref, zsend.at[0], zrecv.at[half * 8 + owner], device(x, y, z_at(d if way == 0 else -d), c))

    def z_wait(owner, half):
        wait_on(half_of(ibig, c * 8 + owner, half), zrecv.at[half * 8 + owner])

    def cross_copy(owner, half):
        ref = half_of(ibig, c * 8 + owner, half)
        copy(ref, ref, isend.at[0], icross.at[half * 8 + owner], twin).start()

    def t_slot(half, u, v):
        return u * 4 + v if half == 0 else v * 4 + u

    def t_here(half):
        return (x, y) if half == 0 else (y, x)

    def t_device(half, u, v):
        return device(u, v, z, c) if half == 0 else device(v, u, z, c)

    def t_send(half, u, v, sem, to_u, to_v):
        ref = half_of(tbig, t_slot(half, u, v), half)
        copy(ref, ref, tsend.at[0], sem.at[half * 4 + u], t_device(half, to_u, to_v)).start()

    def t_wait(half, u, v, sem):
        wait_on(half_of(tbig, t_slot(half, u, v), half), sem.at[half * 4 + u])

    def t_first(half):
        u, v = t_here(half)
        for d in NEAR:
            t_send(half, u, v, tfirst, lax.rem(u + d, 4), v)

    def t_second(half, d):
        u, v = t_here(half)
        there = lax.rem(u + d, 4)
        if d:
            t_wait(half, there, v, tfirst)
        if d == 2:
            t_send(half, there, v, tfar, u, lax.rem(v + 2, 4))
        t_send(half, there, v, tplus, u, lax.rem(v + 1, 4))
        t_send(half, there, v, tminus, u, lax.rem(v + 3, 4))

    def t_pass(half, d):
        u, v = t_here(half)
        there = lax.rem(u + d, 4)
        before = lax.rem(v + 3, 4)
        after = lax.rem(v + 1, 4)
        t_wait(half, there, before, tplus)
        if d < 2:
            t_send(half, there, before, tfar, u, after)
        t_wait(half, there, after, tminus)
        if d == 3:
            t_send(half, there, after, tfar, u, before)

    def t_last(half, d):
        u, v = t_here(half)
        t_wait(half, lax.rem(u + d, 4), lax.rem(v + 2, 4), tfar)

    t_first(0)
    t_first(1)
    z_copy(z, 0, 0).start()
    z_copy(z, 1, 0).start()
    t_second(0, 0)
    t_second(1, 0)
    z_copy(z, 0, 1).start()
    z_copy(z, 1, 1).start()
    cross_copy(z, 0)
    cross_copy(z, 1)
    weights[...] = jnp.zeros_like(weights)
    rsub[...] = jnp.zeros_like(rsub)

    def z_step(step, half):
        left = z_at(-1 - step)
        right = z_at(1 + step)
        z_wait(left, half)
        if step == 1:
            @pl.when(c == 0)
            def _():
                z_copy(left, 0, half, True).start()
        if step < 2:
            z_copy(left, 0, half).start()
        cross_copy(left, half)
        z_wait(right, half)
        if step == 1:
            @pl.when(c == 1)
            def _():
                z_copy(right, 1, half, True).start()
        if step < 2:
            z_copy(right, 1, half).start()
        cross_copy(right, half)

    def t_both(what, d):
        what(0, d)
        what(1, d)

    z_step(0, 0)
    t_both(t_second, 1)
    t_both(t_second, 3)
    z_step(0, 1)
    t_both(t_second, 2)
    z_step(1, 0)
    t_both(t_pass, 0)
    z_step(1, 1)
    t_both(t_pass, 1)
    t_both(t_pass, 3)
    z_step(2, 0)
    z_step(2, 1)
    t_both(t_pass, 2)
    for half in range(2):
        z_wait(z_at(4), half)
        cross_copy(z_at(4), half)
    t_both(t_last, 0)
    t_both(t_last, 1)
    t_both(t_last, 3)
    t_both(t_last, 2)
    text_swap = copy(tbig, tother, xsem.at[0], xsem.at[1], twin)

    def other_image(k, carry):
        wait_on(half_of(ibig, oc * 8 + k, 0), icross.at[k])
        wait_on(half_of(ibig, oc * 8 + k, 1), icross.at[8 + k])
        return carry

    lax.fori_loop(0, 8, other_image, 0)

    scale = scale_ref[0]

    def score(tile, carry):
        cols = pl.ds(pl.multiple_of(tile * WIDE, WIDE), WIDE)
        part = lax.dot_general(
            ibig[...], tbig[cols, :], (((1,), (1,)), ((), ())), preferred_element_type=jnp.float32
        )
        pad = lax.bitwise_and(lax.broadcasted_iota(jnp.int32, (1, WIDE), 1), PITCH - 1) >= ROWS
        logits[:, cols] = jnp.where(pad, FLOOR, part * scale)
        return carry

    lax.fori_loop(0, 4, score, 0)
    text_swap.start()

    def rows_of(k):
        return pl.ds(pl.multiple_of(k * PITCH, PITCH), ROWS)

    cmax[...] = jnp.full_like(cmax, FLOOR)

    def col_max(k, carry):
        cmax[...] = jnp.maximum(cmax[...], jnp.max(logits[rows_of(k), :].reshape(7, 8, TILE), 0))
        return carry

    lax.fori_loop(0, SIDE, col_max, 0)
    col_top = jnp.max(cmax[...], 0, keepdims=True)
    csum[...] = jnp.zeros_like(csum)

    first = lax.broadcasted_iota(jnp.int32, (ROWS, 128), 1) == 0

    def exponentials(g, carry):
        blocks = [rows_of(4 * g + q) for q in range(4)]
        tops = [jnp.max(logits[rows, :], 1, keepdims=True) for rows in blocks]
        added = jnp.zeros((8, TILE), jnp.float32)
        totals = []
        for rows, top in zip(blocks, tops):
            part = logits[rows, :]
            by_row = jnp.exp(part - top)
            by_col = jnp.exp(part - col_top)
            prow[rows, :] = by_row
            pcol[rows, :] = by_col
            added = added + jnp.sum(by_col.reshape(7, 8, TILE), 0)
            totals.append(jnp.sum(by_row, 1, keepdims=True))
        for rows, top, total in zip(blocks, tops, totals):
            rsub[rows, :] = jnp.where(first, top, total)
        csum[...] += added
        return carry

    lax.fori_loop(0, SIDE // 4, exponentials, 0)

    row_stats = jnp.transpose(rsub[...], (1, 0))
    col_total_here = jnp.sum(csum[...], 0, keepdims=True)
    for k in range(4):
        part = slice(k * WIDE, (k + 1) * WIDE)
        rmsg[k:k + 1, :] = row_stats[0:1, part]
        rmsg[4 + k:5 + k, :] = row_stats[1:2, part]
        cmsg[k:k + 1, :] = col_top[:, part]
        cmsg[4 + k:5 + k, :] = col_total_here[:, part]

    def spread(msg, stats, which, mine, peer_of):
        stats[mine] = msg[...]

        def send(k, carry):
            copy(msg, stats.at[mine], small_send.at[which], small_recv.at[which], peer_of(lax.rem(mine + k, SIDE))).start()
            return carry

        lax.fori_loop(1, SIDE, send, 0)

    def collect(stats, which):
        wait_on(stats.at[pl.ds(0, SIDE - 1)], small_recv.at[which])

    spread(rmsg, rstats, 0, islot, row_peer)
    spread(cmsg, cstats, 1, tslot, col_peer)

    def diagonal_slot(k):
        row_block = (x_lo * 2 + lax.div(k, 8)) * 64 + (y * 8 + lax.rem(k, 8)) * 2 + x_hi
        here = jnp.logical_and(lax.rem(row_block, 2) == c, lax.rem(lax.div(row_block, 8), 8) == z)
        slot = (lax.rem(lax.div(row_block, 4), 2) * 2 + lax.rem(lax.div(row_block, 2), 2)) * 4 + lax.div(row_block, 64)
        return here, slot

    def pair_mask(slot):
        row = lax.broadcasted_iota(jnp.int32, (ROWS, 128), 0)
        lane = lax.broadcasted_iota(jnp.int32, (ROWS, 128), 1)
        return lane == row + lax.rem(slot, 2) * PITCH

    def pair_cols(slot):
        return pl.ds(pl.multiple_of(lax.div(slot, 2) * 128, 128), 128)

    dsum[...] = jnp.zeros_like(dsum)

    def diagonal_logits(k, carry):
        here, slot = diagonal_slot(k)

        @pl.when(here)
        def _():
            picked = jnp.where(pair_mask(slot), logits[rows_of(k), pair_cols(slot)], 0.0)
            dsum[...] += jnp.sum(picked.reshape(7, 8, 128), 0)

        return carry

    lax.fori_loop(0, SIDE, diagonal_logits, 0)
    collect(rstats, 0)

    def combine(stats, mine):
        peaks = stats[:, 0:4, :]
        totals = stats[:, 4:8, :]
        peak = jnp.max(peaks, 0)
        total = jnp.sum(totals * jnp.exp(peaks - peak[None]), 0)
        factor = 0.5 * jnp.exp(mine[0:4, :] - peak) / total
        return peak + jnp.log(total), factor

    def line(v):
        return jnp.concatenate([v[k:k + 1, :] for k in range(4)], 1)

    row_lse, row_factor = combine(rstats, rmsg)
    frow[...] = jnp.transpose(jnp.broadcast_to(line(row_factor), (128, TILE)), (1, 0))
    collect(cstats, 1)
    col_lse, col_factor = combine(cstats, cmsg)
    csum[0:1, :] = line(col_factor)

    def weigh(k, carry):
        factor = frow[rows_of(k), :][:, 0:1]
        w = factor * prow[rows_of(k), :] + csum[0:1, :] * pcol[rows_of(k), :]
        weights[rows_of(k), :] = w.astype(jnp.bfloat16)
        here, slot = diagonal_slot(k)

        @pl.when(here)
        def _():
            cols = pair_cols(slot)
            v = frow[rows_of(k), :] * prow[rows_of(k), cols] + csum[0:1, cols] * pcol[rows_of(k), cols]
            v = v - jnp.where(pair_mask(slot), 1.0, 0.0)
            weights[rows_of(k), cols] = v.astype(jnp.bfloat16)

        return carry

    lax.fori_loop(oc * 8, oc * 8 + 8, weigh, 0)
    weight_swap = copy(
        weights.at[pl.ds(pl.multiple_of(oc * CORE, CORE), CORE), :], wother, xsem.at[2], xsem.at[3], twin
    )
    weight_swap.start()
    lax.fori_loop(c * 8, c * 8 + 8, weigh, 0)

    index = lax.broadcasted_iota(jnp.int32, (4, WIDE), 0) * WIDE + lax.broadcasted_iota(jnp.int32, (4, WIDE), 1)
    slot_of = lax.shift_right_logical(index, 6)
    valid = lax.bitwise_and(index, PITCH - 1) < ROWS
    terms = jnp.where(valid & (slot_of == islot), row_lse, 0.0) + jnp.where(valid & (slot_of == tslot), col_lse, 0.0)
    term = jnp.sum(jnp.sum(terms, 0, keepdims=True), 1, keepdims=True)
    diagonal = jnp.sum(jnp.sum(dsum[...], 0, keepdims=True), 1, keepdims=True)
    lmsg[...] = jnp.broadcast_to(term - 2.0 * diagonal, (8, 128))
    spread(lmsg, lstats, 2, islot, row_peer)

    for k in range(TILE // 128):
        wturned[:, k * 128:(k + 1) * 128] = jnp.transpose(weights[k * 128:(k + 1) * 128, :], (1, 0))

    def first_peer(axis, f):
        return device(x, f, z, c) if axis == 0 else device(f, y, z, c)

    def second_peer(axis, s):
        return device(s, y, z, c) if axis == 0 else device(x, s, z, c)

    def slab_copy(p, d):
        axis, _, width, at = PIECES[p]
        me = y if axis == 0 else x
        there = lax.rem(me + d, 4)
        cols = pl.ds(at, width)
        return copy(
            sout.at[axis, there, :, :, cols], sin.at[axis, d - 1, :, :, cols],
            ssend.at[0], srecv.at[p], first_peer(axis, there),
        )

    def text_terms(n):
        low = n * WIDE
        tpart[:, low:low + WIDE] = jnp.dot(wturned[...], ibig[:, low:low + WIDE], preferred_element_type=jnp.float32)
        for p, (axis, col, width, at) in enumerate(PIECES):
            if col // WIDE != n:
                continue
            for m in range(SIDE):
                first, second = (m % 4, m // 4) if axis == 0 else (m // 4, m % 4)
                piece = tpart[m * PITCH:m * PITCH + ROWS, col:col + width]
                sout[axis, first, second, :, at:at + width] = piece.astype(jnp.bfloat16)
            for d in (2, 1, 3):
                slab_copy(p, d).start()

    def keep_copy(p, d):
        axis, _, width, at = PIECES[p]
        me = x if axis == 0 else y
        there = lax.rem(me + d, 4)
        cols = pl.ds(at, width)
        return copy(
            pout.at[axis, there, :, cols], pin.at[axis, d - 1, :, cols],
            psend.at[0], precv.at[p], second_peer(axis, there),
        )

    def text_second(p):
        axis, col, width, at = PIECES[p]
        wait_on(sin.at[axis, pl.ds(0, 3), :, :, pl.ds(at, width)], srecv.at[p])
        me = x if axis == 0 else y
        for d in (2, 1, 3, 0):
            s = lax.rem(me + d, 4)
            m = s * 4 + y if axis == 0 else x * 4 + s
            total = tpart[rows_of(m), col:col + width]
            for e in range(3):
                total = total + sin[axis, e, s, :, at:at + width].astype(jnp.float32)
            if d == 0:
                pkeep[:, col:col + width] = total
            else:
                pout[axis, s, :, at:at + width] = total.astype(jnp.bfloat16)
                keep_copy(p, d).start()

    def text_last(p):
        axis, col, width, at = PIECES[p]
        wait_on(pin.at[axis, pl.ds(0, 3), :, pl.ds(at, width)], precv.at[p])
        total = pkeep[:, col:col + width]
        for d in range(3):
            total = total + pin[axis, d, :, at:at + width].astype(jnp.float32)
        tgrad_ref[:, col:col + width] = total

    def image_send(n, src, slot, low, width, sem, d):
        return copy(
            src, zin.at[slot, :, pl.ds(low, width)], zosend.at[0], sem.at[n], device(x, y, z_at(d), c)
        )

    def image_terms(n):
        low = n * WIDE
        cols = pl.ds(low, WIDE)
        mine = pl.ds(pl.multiple_of(c * CORE, CORE), CORE)
        part = jnp.dot(weights[mine, :], tbig[:, cols], preferred_element_type=jnp.float32)
        ipart[:, cols] = part + jnp.dot(wother[...], tother[:, cols], preferred_element_type=jnp.float32)
        for d in (3, -3, 4, 1, -1):
            zout[z_at(d), :, cols] = ipart[rows_of(z_at(d)), cols].astype(jnp.bfloat16)
        image_send(n, zout.at[z_at(4), :, pl.ds(low, 128)], 2, low, 128, zfirst, 2).start()
        image_send(n, zout.at[z_at(4), :, pl.ds(low + 128, 128)], 2, low + 128, 128, zfirst, -2).start()
        image_send(n, zout.at[z_at(3), :, cols], 0, low, WIDE, zfirst, 1).start()
        image_send(n, zout.at[z_at(-3), :, cols], 1, low, WIDE, zfirst, -1).start()

    def image_near(n):
        low = n * WIDE
        cols = pl.ds(low, WIDE)
        image_send(n, zout.at[z_at(1), :, cols], 3, low, WIDE, zlast, 1).start()
        image_send(n, zout.at[z_at(-1), :, cols], 4, low, WIDE, zlast, -1).start()

    def image_second(n):
        low = n * WIDE
        cols = pl.ds(low, WIDE)
        wait_on(zin.at[pl.ds(0, 3), :, cols], zfirst.at[n])
        for way in range(2):
            d = 2 if way == 0 else -2
            total = ipart[rows_of(z_at(d)), cols] + zin[way, :, cols].astype(jnp.float32)
            edge = low + way * 128
            side = total[:, way * 128:way * 128 + 128] + zin[2, :, edge:edge + 128].astype(jnp.float32)
            rest = low + 128 - way * 128
            zagg[way, :, edge:edge + 128] = side.astype(jnp.bfloat16)
            zagg[way, :, rest:rest + 128] = total[:, 128 - way * 128:256 - way * 128].astype(jnp.bfloat16)
            image_send(n, zagg.at[way, :, cols], 5 + way, low, WIDE, zlast, d).start()

    def image_last(n):
        cols = pl.ds(n * WIDE, WIDE)
        wait_on(zin.at[pl.ds(3, 4), :, cols], zlast.at[n])
        total = ipart[rows_of(z), cols]
        for k in range(3, 7):
            total = total + zin[k, :, cols].astype(jnp.float32)
        igrad_ref[:, cols] = total

    def both_second(n):
        image_second(n)
        image_near(n)

    def text_both(n):
        text_second(2 * n)
        text_second(2 * n + 1)

    text_terms(0)
    text_swap.wait()
    weight_swap.wait()
    image_terms(0)
    text_terms(1)
    image_terms(1)
    both_second(0)
    text_terms(2)
    image_terms(2)
    text_both(0)
    both_second(1)
    text_terms(3)
    image_terms(3)
    text_both(1)
    both_second(2)
    text_terms(4)
    image_terms(4)
    text_both(2)
    both_second(3)
    collect(lstats, 2)
    pmsg[...] = jnp.sum(lstats[...], 0)
    spread(pmsg, pstats, 3, tslot, col_peer)
    both_second(4)
    text_both(3)
    text_both(4)
    for n in range(CHUNKS):
        image_last(n)
        text_last(2 * n)
        text_last(2 * n + 1)
    collect(pstats, 3)
    loss_ref[...] = (jnp.sum(pstats[...], 0) / (2.0 * PAIRS))[0:1, 0:1]

    wait_on(ibig.at[pl.ds(0, 7 * PITCH), :], zsend.at[0])
    wait_on(ibig.at[pl.ds(0, 8 * PITCH), :], isend.at[0])
    wait_on(tbig.at[pl.ds(0, 15 * PITCH), :], tsend.at[0])
    wait_on(rstats.at[pl.ds(0, SIDE - 1)], small_send.at[0])
    wait_on(cstats.at[pl.ds(0, SIDE - 1)], small_send.at[1])
    wait_on(lstats.at[pl.ds(0, SIDE - 1)], small_send.at[2])
    wait_on(pstats.at[pl.ds(0, SIDE - 1)], small_send.at[3])
    wait_on(zin, zosend.at[0])
    wait_on(sout.at[:, pl.ds(0, 3)], ssend.at[0])
    wait_on(pout.at[:, pl.ds(0, 3)], psend.at[0])


def per_device(images, texts, logit_scale):
    f32, bf16 = jnp.float32, jnp.bfloat16
    dma = pltpu.SemaphoreType.DMA
    vmem = pl.BlockSpec(memory_space=pltpu.VMEM)
    smem = pl.BlockSpec(memory_space=pltpu.SMEM)
    hbm = pl.BlockSpec(memory_space=pl.ANY)
    loss, image_grad, text_grad = pl.pallas_call(
        kernel,
        out_shape=(
            jax.ShapeDtypeStruct((1, 1), f32),
            jax.ShapeDtypeStruct((ROWS, E), f32),
            jax.ShapeDtypeStruct((ROWS, E), f32),
        ),
        in_specs=[hbm, hbm, smem],
        out_specs=(vmem, vmem, vmem),
        scratch_shapes=[
            pltpu.VMEM((2, ROWS, E), bf16),
            pltpu.VMEM((TILE, E), bf16),
            pltpu.VMEM((TILE, E), bf16),
            pltpu.VMEM((TILE, E), bf16),
            pltpu.VMEM((TILE, TILE), f32),
            pltpu.VMEM((TILE, TILE), f32),
            pltpu.VMEM((TILE, TILE), f32),
            pltpu.VMEM((TILE, TILE), bf16),
            pltpu.VMEM((CORE, TILE), bf16),
            pltpu.VMEM((TILE, TILE), bf16),
            pltpu.VMEM((TILE, 128), f32),
            pltpu.VMEM((8, TILE), f32),
            pltpu.VMEM((8, TILE), f32),
            pltpu.VMEM((8, 128), f32),
            pltpu.VMEM((TILE, 128), f32),
            pltpu.VMEM((8, WIDE), f32),
            pltpu.VMEM((8, WIDE), f32),
            pltpu.VMEM((SIDE, 8, WIDE), f32),
            pltpu.VMEM((SIDE, 8, WIDE), f32),
            pltpu.VMEM((8, 128), f32),
            pltpu.VMEM((SIDE, 8, 128), f32),
            pltpu.VMEM((8, 128), f32),
            pltpu.VMEM((SIDE, 8, 128), f32),
            pltpu.VMEM((CORE, E), f32),
            pltpu.VMEM((TILE, E), f32),
            pltpu.VMEM((8, ROWS, E), bf16),
            pltpu.VMEM((2, ROWS, E), bf16),
            pltpu.VMEM((7, ROWS, E), bf16),
            pltpu.VMEM((2, 4, 4, ROWS, HALF), bf16),
            pltpu.VMEM((2, 3, 4, ROWS, HALF), bf16),
            pltpu.VMEM((2, 4, ROWS, HALF), bf16),
            pltpu.VMEM((2, 3, ROWS, HALF), bf16),
            pltpu.VMEM((ROWS, E), f32),
            dma((2,)), dma((1,)), dma((16,)), dma((1,)), dma((16,)),
            dma((1,)), dma((8,)), dma((8,)), dma((8,)), dma((8,)), dma((4,)),
            dma((4,)), dma((4,)), dma((1,)), dma((5,)), dma((5,)),
            dma((1,)), dma((10,)), dma((1,)), dma((10,)),
        ],
        compiler_params=pltpu.CompilerParams(
            collective_id=0, has_side_effects=True, vmem_limit_bytes=60 * 1024 * 1024
        ),
    )(images, texts, logit_scale)
    return loss.reshape(1), image_grad, text_grad


def solution(mesh):
    in_specs = (P(("img", "txt"), None), P(("txt", "img"), None), P())
    out_specs = (P(), P(("img", "txt"), None), P(("txt", "img"), None))
    return jax.shard_map(
        per_device, mesh=mesh, in_specs=in_specs, out_specs=out_specs, check_vma=False
    )
```

```python
import jax
import jax.numpy as jnp
from jax import lax
from jax.experimental import pallas as pl
from jax.experimental.pallas import tpu as pltpu
from jax.sharding import PartitionSpec as P

MESH = pl.DeviceIdType.MESH
ROWS = 56
PITCH = 64
SIDE = 16
TILE = SIDE * PITCH
CORE = 8 * PITCH
E = 1280
PAIRS = 14336
WIDE = 256
CHUNKS = E // WIDE
HALF = 640
FLOOR = -1e30
PIECES = tuple(
    (axis, n * WIDE + axis * 128, 128, n * 128) for n in range(CHUNKS) for axis in range(2)
)
NEAR = (1, 3, 2)


def device(x, y, z, c):
    return (lax.rem(x, 2) * 2 + c, (y * 8 + z) * 2 + lax.div(x, 2))


def kernel(
    images_ref, texts_ref, scale_ref,
    loss_ref, igrad_ref, tgrad_ref,
    stage, ibig, tbig, tother, logits, prow, pcol, weights, wother, wturned,
    rsub, csum, cmax, dsum, frow, rmsg, cmsg, rstats, cstats, lmsg, lstats, pmsg, pstats,
    ipart, tpart, zout, zagg, zin, sout, sin, pout, pin, pkeep,
    own_sem, zsend, zrecv, isend, icross, tsend, tfirst, tplus, tminus, tfar, xsem,
    small_send, small_recv, zosend, zfirst, zlast, ssend, srecv, psend, precv,
):
    img = lax.axis_index("img")
    txt = lax.axis_index("txt")
    x_lo = lax.div(img, 2)
    c = lax.rem(img, 2)
    x_hi = lax.rem(txt, 2)
    x = x_hi * 2 + x_lo
    y = lax.div(txt, 16)
    z = lax.rem(lax.div(txt, 2), 8)
    oc = 1 - c
    islot = c * 8 + z
    tslot = x * 4 + y

    def x_at(d):
        return lax.rem(x + d, 4)

    def y_at(d):
        return lax.rem(y + d, 4)

    def z_at(d):
        return lax.rem(z + d + 8, 8)

    def row_peer(slot):
        return device(x, y, lax.rem(slot, 8), lax.div(slot, 8))

    def col_peer(slot):
        return device(lax.div(slot, 4), lax.rem(slot, 4), z, c)

    twin = device(x, y, z, oc)

    def copy(src, dst, send, recv, where):
        return pltpu.make_async_remote_copy(
            src_ref=src, dst_ref=dst, send_sem=send, recv_sem=recv,
            device_id=where, device_id_type=MESH,
        )

    def wait_on(ref, sem):
        copy(ref, ref, sem, sem, twin).wait_recv()

    barrier = pltpu.get_barrier_semaphore()

    def greet(k, carry):
        pl.semaphore_signal(barrier, inc=1, device_id=row_peer(lax.rem(islot + k, SIDE)), device_id_type=MESH)
        pl.semaphore_signal(barrier, inc=1, device_id=col_peer(lax.rem(tslot + k, SIDE)), device_id_type=MESH)
        return carry

    lax.fori_loop(1, SIDE, greet, 0)
    own_image = pltpu.make_async_copy(images_ref, stage.at[0], own_sem.at[0])
    own_text = pltpu.make_async_copy(texts_ref, stage.at[1], own_sem.at[1])
    own_image.start()
    own_text.start()

    def block_rows(slot):
        return pl.ds(pl.multiple_of(slot * PITCH, PITCH), PITCH)

    ibig[block_rows(islot), :] = jnp.zeros((PITCH, E), jnp.bfloat16)
    tbig[block_rows(tslot), :] = jnp.zeros((PITCH, E), jnp.bfloat16)
    own_image.wait()
    own_text.wait()
    ibig[pl.ds(pl.multiple_of(islot * PITCH, PITCH), ROWS), :] = stage[0]
    tbig[pl.ds(pl.multiple_of(tslot * PITCH, PITCH), ROWS), :] = stage[1]
    pl.semaphore_wait(barrier, 2 * (SIDE - 1))

    def half_of(big, slot, half):
        return big.at[block_rows(slot), pl.ds(half * HALF, HALF)]

    def z_copy(owner, way, half, far=False):
        ref = half_of(ibig, c * 8 + owner, half)
        d = 2 if far else 1
        return copy(ref, ref, zsend.at[0], zrecv.at[half * 8 + owner], device(x, y, z_at(d if way == 0 else -d), c))

    def z_wait(owner, half):
        wait_on(half_of(ibig, c * 8 + owner, half), zrecv.at[half * 8 + owner])

    def cross_copy(owner, half):
        ref = half_of(ibig, c * 8 + owner, half)
        copy(ref, ref, isend.at[0], icross.at[half * 8 + owner], twin).start()

    def t_slot(half, u, v):
        return u * 4 + v if half == 0 else v * 4 + u

    def t_here(half):
        return (x, y) if half == 0 else (y, x)

    def t_device(half, u, v):
        return device(u, v, z, c) if half == 0 else device(v, u, z, c)

    def t_send(half, u, v, sem, to_u, to_v):
        ref = half_of(tbig, t_slot(half, u, v), half)
        copy(ref, ref, tsend.at[0], sem.at[half * 4 + u], t_device(half, to_u, to_v)).start()

    def t_wait(half, u, v, sem):
        wait_on(half_of(tbig, t_slot(half, u, v), half), sem.at[half * 4 + u])

    def t_first(half):
        u, v = t_here(half)
        for d in NEAR:
            t_send(half, u, v, tfirst, lax.rem(u + d, 4), v)

    def t_second(half, d):
        u, v = t_here(half)
        there = lax.rem(u + d, 4)
        if d:
            t_wait(half, there, v, tfirst)
        if d == 2:
            t_send(half, there, v, tfar, u, lax.rem(v + 2, 4))
        t_send(half, there, v, tplus, u, lax.rem(v + 1, 4))
        t_send(half, there, v, tminus, u, lax.rem(v + 3, 4))

    def t_pass(half, d):
        u, v = t_here(half)
        there = lax.rem(u + d, 4)
        before = lax.rem(v + 3, 4)
        after = lax.rem(v + 1, 4)
        t_wait(half, there, before, tplus)
        if d < 2:
            t_send(half, there, before, tfar, u, after)
        t_wait(half, there, after, tminus)
        if d == 3:
            t_send(half, there, after, tfar, u, before)

    def t_last(half, d):
        u, v = t_here(half)
        t_wait(half, lax.rem(u + d, 4), lax.rem(v + 2, 4), tfar)

    t_first(0)
    t_first(1)
    z_copy(z, 0, 0).start()
    z_copy(z, 1, 0).start()
    t_second(0, 0)
    t_second(1, 0)
    z_copy(z, 0, 1).start()
    z_copy(z, 1, 1).start()
    cross_copy(z, 0)
    cross_copy(z, 1)
    weights[...] = jnp.zeros_like(weights)
    rsub[...] = jnp.zeros_like(rsub)

    def z_step(step, half):
        left = z_at(-1 - step)
        right = z_at(1 + step)
        z_wait(left, half)
        if step == 1:
            @pl.when(c == 0)
            def _():
                z_copy(left, 0, half, True).start()
        if step < 2:
            z_copy(left, 0, half).start()
        cross_copy(left, half)
        z_wait(right, half)
        if step == 1:
            @pl.when(c == 1)
            def _():
                z_copy(right, 1, half, True).start()
        if step < 2:
            z_copy(right, 1, half).start()
        cross_copy(right, half)

    def t_both(what, d):
        what(0, d)
        what(1, d)

    z_step(0, 0)
    t_both(t_second, 1)
    t_both(t_second, 3)
    z_step(0, 1)
    t_both(t_second, 2)
    z_step(1, 0)
    t_both(t_pass, 0)
    z_step(1, 1)
    t_both(t_pass, 1)
    t_both(t_pass, 3)
    z_step(2, 0)
    z_step(2, 1)
    t_both(t_pass, 2)
    for half in range(2):
        z_wait(z_at(4), half)
        cross_copy(z_at(4), half)
    t_both(t_last, 0)
    t_both(t_last, 1)
    t_both(t_last, 3)
    t_both(t_last, 2)
    scale = scale_ref[0]

    def score(tile, lane_rows):
        cols = pl.ds(pl.multiple_of(tile * WIDE, WIDE), WIDE)
        rows = pl.ds(pl.multiple_of(lane_rows, CORE), CORE)
        part = lax.dot_general(
            ibig[rows, :], tbig[cols, :], (((1,), (1,)), ((), ())), preferred_element_type=jnp.float32
        )
        pad = lax.bitwise_and(lax.broadcasted_iota(jnp.int32, (1, WIDE), 1), PITCH - 1) >= ROWS
        logits[rows, cols] = jnp.where(pad, FLOOR, part * scale)
        return lane_rows

    def other_image(k, carry):
        wait_on(half_of(ibig, oc * 8 + k, 0), icross.at[k])
        wait_on(half_of(ibig, oc * 8 + k, 1), icross.at[8 + k])
        return carry

    lax.fori_loop(0, 4, score, c * CORE)
    lax.fori_loop(0, 8, other_image, 0)
    lax.fori_loop(0, 4, score, oc * CORE)
    text_swap = copy(tbig, tother, xsem.at[0], xsem.at[1], twin)
    text_swap.start()

    def rows_of(k):
        return pl.ds(pl.multiple_of(k * PITCH, PITCH), ROWS)

    cmax[...] = jnp.full_like(cmax, FLOOR)
    first = lax.broadcasted_iota(jnp.int32, (ROWS, 128), 1) == 0

    def four(g):
        return [rows_of(4 * g + q) for q in range(4)]

    def row_part(g, carry):
        tops = []
        peak = cmax[...]
        for rows in four(g):
            part = logits[rows, :]
            tops.append(jnp.max(part, 1, keepdims=True))
            peak = jnp.maximum(peak, jnp.max(part.reshape(7, 8, TILE), 0))
        totals = []
        for rows, top in zip(four(g), tops):
            by_row = jnp.exp(logits[rows, :] - top)
            prow[rows, :] = by_row
            totals.append(jnp.sum(by_row, 1, keepdims=True))
        for rows, top, total in zip(four(g), tops, totals):
            rsub[rows, :] = jnp.where(first, top, total)
        cmax[...] = peak
        return carry

    lax.fori_loop(0, SIDE // 4, row_part, 0)

    def spread(msg, stats, which, mine, peer_of):
        stats[mine] = msg[...]

        def send(k, carry):
            copy(msg, stats.at[mine], small_send.at[which], small_recv.at[which], peer_of(lax.rem(mine + k, SIDE))).start()
            return carry

        lax.fori_loop(1, SIDE, send, 0)

    def collect(stats, which):
        wait_on(stats.at[pl.ds(0, SIDE - 1)], small_recv.at[which])

    row_stats = jnp.transpose(rsub[...], (1, 0))
    for k in range(4):
        part = slice(k * WIDE, (k + 1) * WIDE)
        rmsg[k:k + 1, :] = row_stats[0:1, part]
        rmsg[4 + k:5 + k, :] = row_stats[1:2, part]
    spread(rmsg, rstats, 0, islot, row_peer)

    col_top = jnp.max(cmax[...], 0, keepdims=True)
    csum[...] = jnp.zeros_like(csum)

    def col_part(g, carry):
        added = csum[...]
        for rows in four(g):
            by_col = jnp.exp(logits[rows, :] - col_top)
            pcol[rows, :] = by_col
            added = added + jnp.sum(by_col.reshape(7, 8, TILE), 0)
        csum[...] = added
        return carry

    lax.fori_loop(0, SIDE // 4, col_part, 0)
    col_total_here = jnp.sum(csum[...], 0, keepdims=True)
    for k in range(4):
        part = slice(k * WIDE, (k + 1) * WIDE)
        cmsg[k:k + 1, :] = col_top[:, part]
        cmsg[4 + k:5 + k, :] = col_total_here[:, part]
    spread(cmsg, cstats, 1, tslot, col_peer)

    def diagonal_slot(k):
        row_block = (x_lo * 2 + lax.div(k, 8)) * 64 + (y * 8 + lax.rem(k, 8)) * 2 + x_hi
        here = jnp.logical_and(lax.rem(row_block, 2) == c, lax.rem(lax.div(row_block, 8), 8) == z)
        slot = (lax.rem(lax.div(row_block, 4), 2) * 2 + lax.rem(lax.div(row_block, 2), 2)) * 4 + lax.div(row_block, 64)
        return here, slot

    def pair_mask(slot):
        row = lax.broadcasted_iota(jnp.int32, (ROWS, 128), 0)
        lane = lax.broadcasted_iota(jnp.int32, (ROWS, 128), 1)
        return lane == row + lax.rem(slot, 2) * PITCH

    def pair_cols(slot):
        return pl.ds(pl.multiple_of(lax.div(slot, 2) * 128, 128), 128)

    dsum[...] = jnp.zeros_like(dsum)

    def diagonal_logits(k, carry):
        here, slot = diagonal_slot(k)

        @pl.when(here)
        def _():
            picked = jnp.where(pair_mask(slot), logits[rows_of(k), pair_cols(slot)], 0.0)
            dsum[...] += jnp.sum(picked.reshape(7, 8, 128), 0)

        return carry

    lax.fori_loop(0, SIDE, diagonal_logits, 0)
    collect(rstats, 0)

    def combine(stats, mine):
        peaks = stats[:, 0:4, :]
        totals = stats[:, 4:8, :]
        peak = jnp.max(peaks, 0)
        total = jnp.sum(totals * jnp.exp(peaks - peak[None]), 0)
        factor = 0.5 * jnp.exp(mine[0:4, :] - peak) / total
        return peak + jnp.log(total), factor

    def line(v):
        return jnp.concatenate([v[k:k + 1, :] for k in range(4)], 1)

    row_lse, row_factor = combine(rstats, rmsg)
    frow[...] = jnp.transpose(jnp.broadcast_to(line(row_factor), (128, TILE)), (1, 0))
    collect(cstats, 1)
    col_lse, col_factor = combine(cstats, cmsg)
    csum[0:1, :] = line(col_factor)

    def weigh(k, carry):
        factor = frow[rows_of(k), :][:, 0:1]
        w = factor * prow[rows_of(k), :] + csum[0:1, :] * pcol[rows_of(k), :]
        weights[rows_of(k), :] = w.astype(jnp.bfloat16)
        here, slot = diagonal_slot(k)

        @pl.when(here)
        def _():
            cols = pair_cols(slot)
            v = frow[rows_of(k), :] * prow[rows_of(k), cols] + csum[0:1, cols] * pcol[rows_of(k), cols]
            v = v - jnp.where(pair_mask(slot), 1.0, 0.0)
            weights[rows_of(k), cols] = v.astype(jnp.bfloat16)

        return carry

    lax.fori_loop(oc * 8, oc * 8 + 8, weigh, 0)
    weight_swap = copy(
        weights.at[pl.ds(pl.multiple_of(oc * CORE, CORE), CORE), :], wother, xsem.at[2], xsem.at[3], twin
    )
    weight_swap.start()
    lax.fori_loop(c * 8, c * 8 + 8, weigh, 0)

    index = lax.broadcasted_iota(jnp.int32, (4, WIDE), 0) * WIDE + lax.broadcasted_iota(jnp.int32, (4, WIDE), 1)
    slot_of = lax.shift_right_logical(index, 6)
    valid = lax.bitwise_and(index, PITCH - 1) < ROWS
    terms = jnp.where(valid & (slot_of == islot), row_lse, 0.0) + jnp.where(valid & (slot_of == tslot), col_lse, 0.0)
    term = jnp.sum(jnp.sum(terms, 0, keepdims=True), 1, keepdims=True)
    diagonal = jnp.sum(jnp.sum(dsum[...], 0, keepdims=True), 1, keepdims=True)
    lmsg[...] = jnp.broadcast_to(term - 2.0 * diagonal, (8, 128))
    spread(lmsg, lstats, 2, islot, row_peer)

    for k in range(TILE // 128):
        wturned[:, k * 128:(k + 1) * 128] = jnp.transpose(weights[k * 128:(k + 1) * 128, :], (1, 0))

    def first_peer(axis, f):
        return device(x, f, z, c) if axis == 0 else device(f, y, z, c)

    def second_peer(axis, s):
        return device(s, y, z, c) if axis == 0 else device(x, s, z, c)

    def slab_copy(p, d):
        axis, _, width, at = PIECES[p]
        me = y if axis == 0 else x
        there = lax.rem(me + d, 4)
        cols = pl.ds(at, width)
        return copy(
            sout.at[axis, there, :, :, cols], sin.at[axis, d - 1, :, :, cols],
            ssend.at[0], srecv.at[p], first_peer(axis, there),
        )

    def text_terms(n):
        low = n * WIDE
        tpart[:, low:low + WIDE] = jnp.dot(wturned[...], ibig[:, low:low + WIDE], preferred_element_type=jnp.float32)
        for p, (axis, col, width, at) in enumerate(PIECES):
            if col // WIDE != n:
                continue
            for m in range(SIDE):
                first, second = (m % 4, m // 4) if axis == 0 else (m // 4, m % 4)
                piece = tpart[m * PITCH:m * PITCH + ROWS, col:col + width]
                sout[axis, first, second, :, at:at + width] = piece.astype(jnp.bfloat16)
            for d in (2, 1, 3):
                slab_copy(p, d).start()

    def keep_copy(p, d):
        axis, _, width, at = PIECES[p]
        me = x if axis == 0 else y
        there = lax.rem(me + d, 4)
        cols = pl.ds(at, width)
        return copy(
            pout.at[axis, there, :, cols], pin.at[axis, d - 1, :, cols],
            psend.at[0], precv.at[p], second_peer(axis, there),
        )

    def text_second(p):
        axis, col, width, at = PIECES[p]
        wait_on(sin.at[axis, pl.ds(0, 3), :, :, pl.ds(at, width)], srecv.at[p])
        me = x if axis == 0 else y
        for d in (2, 1, 3, 0):
            s = lax.rem(me + d, 4)
            m = s * 4 + y if axis == 0 else x * 4 + s
            total = tpart[rows_of(m), col:col + width]
            for e in range(3):
                total = total + sin[axis, e, s, :, at:at + width].astype(jnp.float32)
            if d == 0:
                pkeep[:, col:col + width] = total
            else:
                pout[axis, s, :, at:at + width] = total.astype(jnp.bfloat16)
                keep_copy(p, d).start()

    def text_last(p):
        axis, col, width, at = PIECES[p]
        wait_on(pin.at[axis, pl.ds(0, 3), :, pl.ds(at, width)], precv.at[p])
        total = pkeep[:, col:col + width]
        for d in range(3):
            total = total + pin[axis, d, :, at:at + width].astype(jnp.float32)
        tgrad_ref[:, col:col + width] = total

    def image_send(n, src, slot, low, width, sem, d):
        return copy(
            src, zin.at[slot, :, pl.ds(low, width)], zosend.at[0], sem.at[n], device(x, y, z_at(d), c)
        )

    def image_terms(n):
        low = n * WIDE
        cols = pl.ds(low, WIDE)
        mine = pl.ds(pl.multiple_of(c * CORE, CORE), CORE)
        part = jnp.dot(weights[mine, :], tbig[:, cols], preferred_element_type=jnp.float32)
        ipart[:, cols] = part + jnp.dot(wother[...], tother[:, cols], preferred_element_type=jnp.float32)
        for d in (3, -3, 4, 1, -1):
            zout[z_at(d), :, cols] = ipart[rows_of(z_at(d)), cols].astype(jnp.bfloat16)
        image_send(n, zout.at[z_at(4), :, pl.ds(low, 128)], 2, low, 128, zfirst, 2).start()
        image_send(n, zout.at[z_at(4), :, pl.ds(low + 128, 128)], 2, low + 128, 128, zfirst, -2).start()
        image_send(n, zout.at[z_at(3), :, cols], 0, low, WIDE, zfirst, 1).start()
        image_send(n, zout.at[z_at(-3), :, cols], 1, low, WIDE, zfirst, -1).start()

    def image_near(n):
        low = n * WIDE
        cols = pl.ds(low, WIDE)
        image_send(n, zout.at[z_at(1), :, cols], 3, low, WIDE, zlast, 1).start()
        image_send(n, zout.at[z_at(-1), :, cols], 4, low, WIDE, zlast, -1).start()

    def image_second(n):
        low = n * WIDE
        cols = pl.ds(low, WIDE)
        wait_on(zin.at[pl.ds(0, 3), :, cols], zfirst.at[n])
        for way in range(2):
            d = 2 if way == 0 else -2
            total = ipart[rows_of(z_at(d)), cols] + zin[way, :, cols].astype(jnp.float32)
            edge = low + way * 128
            side = total[:, way * 128:way * 128 + 128] + zin[2, :, edge:edge + 128].astype(jnp.float32)
            rest = low + 128 - way * 128
            zagg[way, :, edge:edge + 128] = side.astype(jnp.bfloat16)
            zagg[way, :, rest:rest + 128] = total[:, 128 - way * 128:256 - way * 128].astype(jnp.bfloat16)
            image_send(n, zagg.at[way, :, cols], 5 + way, low, WIDE, zlast, d).start()

    def image_last(n):
        cols = pl.ds(n * WIDE, WIDE)
        wait_on(zin.at[pl.ds(3, 4), :, cols], zlast.at[n])
        total = ipart[rows_of(z), cols]
        for k in range(3, 7):
            total = total + zin[k, :, cols].astype(jnp.float32)
        igrad_ref[:, cols] = total

    def both_second(n):
        image_second(n)
        image_near(n)

    def text_both(n):
        text_second(2 * n)
        text_second(2 * n + 1)

    text_terms(0)
    text_swap.wait()
    weight_swap.wait()
    image_terms(0)
    text_terms(1)
    image_terms(1)
    both_second(0)
    text_terms(2)
    image_terms(2)
    text_both(0)
    both_second(1)
    text_terms(3)
    image_terms(3)
    text_both(1)
    both_second(2)
    text_terms(4)
    image_terms(4)
    text_both(2)
    both_second(3)
    collect(lstats, 2)
    pmsg[...] = jnp.sum(lstats[...], 0)
    spread(pmsg, pstats, 3, tslot, col_peer)
    both_second(4)
    text_both(3)
    text_both(4)
    for n in range(CHUNKS):
        image_last(n)
        text_last(2 * n)
        text_last(2 * n + 1)
    collect(pstats, 3)
    loss_ref[...] = (jnp.sum(pstats[...], 0) / (2.0 * PAIRS))[0:1, 0:1]

    wait_on(ibig.at[pl.ds(0, 7 * PITCH), :], zsend.at[0])
    wait_on(ibig.at[pl.ds(0, 8 * PITCH), :], isend.at[0])
    wait_on(tbig.at[pl.ds(0, 15 * PITCH), :], tsend.at[0])
    wait_on(rstats.at[pl.ds(0, SIDE - 1)], small_send.at[0])
    wait_on(cstats.at[pl.ds(0, SIDE - 1)], small_send.at[1])
    wait_on(lstats.at[pl.ds(0, SIDE - 1)], small_send.at[2])
    wait_on(pstats.at[pl.ds(0, SIDE - 1)], small_send.at[3])
    wait_on(zin, zosend.at[0])
    wait_on(sout.at[:, pl.ds(0, 3)], ssend.at[0])
    wait_on(pout.at[:, pl.ds(0, 3)], psend.at[0])


def per_device(images, texts, logit_scale):
    f32, bf16 = jnp.float32, jnp.bfloat16
    dma = pltpu.SemaphoreType.DMA
    vmem = pl.BlockSpec(memory_space=pltpu.VMEM)
    smem = pl.BlockSpec(memory_space=pltpu.SMEM)
    hbm = pl.BlockSpec(memory_space=pl.ANY)
    loss, image_grad, text_grad = pl.pallas_call(
        kernel,
        out_shape=(
            jax.ShapeDtypeStruct((1, 1), f32),
            jax.ShapeDtypeStruct((ROWS, E), f32),
            jax.ShapeDtypeStruct((ROWS, E), f32),
        ),
        in_specs=[hbm, hbm, smem],
        out_specs=(vmem, vmem, vmem),
        scratch_shapes=[
            pltpu.VMEM((2, ROWS, E), bf16),
            pltpu.VMEM((TILE, E), bf16),
            pltpu.VMEM((TILE, E), bf16),
            pltpu.VMEM((TILE, E), bf16),
            pltpu.VMEM((TILE, TILE), f32),
            pltpu.VMEM((TILE, TILE), f32),
            pltpu.VMEM((TILE, TILE), f32),
            pltpu.VMEM((TILE, TILE), bf16),
            pltpu.VMEM((CORE, TILE), bf16),
            pltpu.VMEM((TILE, TILE), bf16),
            pltpu.VMEM((TILE, 128), f32),
            pltpu.VMEM((8, TILE), f32),
            pltpu.VMEM((8, TILE), f32),
            pltpu.VMEM((8, 128), f32),
            pltpu.VMEM((TILE, 128), f32),
            pltpu.VMEM((8, WIDE), f32),
            pltpu.VMEM((8, WIDE), f32),
            pltpu.VMEM((SIDE, 8, WIDE), f32),
            pltpu.VMEM((SIDE, 8, WIDE), f32),
            pltpu.VMEM((8, 128), f32),
            pltpu.VMEM((SIDE, 8, 128), f32),
            pltpu.VMEM((8, 128), f32),
            pltpu.VMEM((SIDE, 8, 128), f32),
            pltpu.VMEM((CORE, E), f32),
            pltpu.VMEM((TILE, E), f32),
            pltpu.VMEM((8, ROWS, E), bf16),
            pltpu.VMEM((2, ROWS, E), bf16),
            pltpu.VMEM((7, ROWS, E), bf16),
            pltpu.VMEM((2, 4, 4, ROWS, HALF), bf16),
            pltpu.VMEM((2, 3, 4, ROWS, HALF), bf16),
            pltpu.VMEM((2, 4, ROWS, HALF), bf16),
            pltpu.VMEM((2, 3, ROWS, HALF), bf16),
            pltpu.VMEM((ROWS, E), f32),
            dma((2,)), dma((1,)), dma((16,)), dma((1,)), dma((16,)),
            dma((1,)), dma((8,)), dma((8,)), dma((8,)), dma((8,)), dma((4,)),
            dma((4,)), dma((4,)), dma((1,)), dma((5,)), dma((5,)),
            dma((1,)), dma((10,)), dma((1,)), dma((10,)),
        ],
        compiler_params=pltpu.CompilerParams(
            collective_id=0, has_side_effects=True, vmem_limit_bytes=60 * 1024 * 1024
        ),
    )(images, texts, logit_scale)
    return loss.reshape(1), image_grad, text_grad


def solution(mesh):
    in_specs = (P(("img", "txt"), None), P(("txt", "img"), None), P())
    out_specs = (P(), P(("img", "txt"), None), P(("txt", "img"), None))
    return jax.shard_map(
        per_device, mesh=mesh, in_specs=in_specs, out_specs=out_specs, check_vma=False
    )
```
